256 devices in a mesh: grp: 16 (over z, core), tp: 16 (over y, x).
Axes of the slice: x: 4, y: 4, z: 8, core: 2. Of those that a mesh axis runs over, the one named last changes fastest.
Arguments:
- tensor_blocks: bfloat16 [256, 3, 128, 64, 128], P(('grp', 'tp')), may hold values from -6 to 6
- occupied: bfloat16 [256, 3, 128, 128], P('grp'), may hold values from -0.3125 to 0.3125
- virtual: bfloat16 [256, 3, 128, 128], P('grp'), may hold values from -0.3125 to 0.3125
- slot_block: int32 [16, 16], P('grp'), may hold values from 0 to 15, each once within a row
- pair_kept: int32 [256], replicated, may hold values 0 or 1
- block_funcs: int32 [256], replicated, may hold values from 96 to 128
Outputs:
- polarizability: float32 [256, 5, 64, 64], P(('grp', 'tp'))
The draws below stay inside these ranges and needn't reach their ends.
Inputs may be any that keep to these rules, and one draw needn't show every extreme that they name: `slot_block`: each row is a permutation of the region's 16 columns. `pair_kept`: entry j filters the pair of AO blocks j and j + 1 (both orders). `block_funcs`: functions past this count in a block of 128 are padding.
All inputs are finite; a program needn't handle non-finite values.
Results may differ from the reference program's by a relative error of at most 0.0041.
Values may be sent and summed in bfloat16 or wider, within the bound.
A program may use at most 128 MiB of HBM per device.

```python
import jax
import jax.numpy as jnp
from jax import lax

BS = 128
BA = 64
REG = 16
REGIONS = 16
NB = 256


def touch_ends(entries, stream_key, low, largest):
    dims = entries.shape
    index_at = [jax.random.randint(jax.random.fold_in(stream_key, axis), (), 0, dims[axis]) for axis in range(len(dims))]
    entries = entries.at[tuple(index_at)].set(low)
    longest = dims.index(max(dims))
    index_at[longest] = (index_at[longest] + 1) % dims[longest]
    return entries.at[tuple(index_at)].set(largest)


def block_levels(rng, shape, shards, low, largest):
    level, own = 1.0, jax.random.fold_in(rng, 6)
    for dim, parts in shards:
        heights = jnp.exp(jax.random.uniform(jax.random.fold_in(own, dim), (parts,), jnp.float32, low / len(shards), largest / len(shards)))
        level = level * jnp.repeat(heights, shape[dim] // parts).reshape([-1 if axis == dim else 1 for axis in range(len(shape))])
    return level


def noise(stream_key, dims, deviation, most, cuts=(), held_as=jnp.bfloat16):
    level = block_levels(stream_key, dims, cuts, -0.22, 0.18) if cuts else 1.0
    entries = jax.random.normal(stream_key, dims, jnp.float32) * deviation * level
    return jnp.minimum(jnp.maximum(entries, -most), most).astype(held_as)


def setup_inputs(seed: int = 0) -> dict:
    key_of = jax.random.split(jax.random.key(seed), 7)
    return {
        "tensor_blocks": noise(key_of[0], (NB, 3, BS, BA, BS), 1.0, 6.0, ((0, 256),)),
        "occupied": noise(key_of[1], (NB, 3, BS, BS), (3 * BS) ** -0.5, 0.3125, ((0, 16),)),
        "virtual": noise(key_of[2], (NB, 3, BS, BS), (3 * BS) ** -0.5, 0.3125, ((0, 16),)),
        "slot_block": jax.vmap(lambda own: jax.random.permutation(own, REG))(jax.random.split(key_of[3], REGIONS)).reshape((REGIONS, REG)).astype(jnp.int32),
        "pair_kept": touch_ends((jax.random.randint(key_of[4], (NB,), 0, 4) < 3).astype(jnp.int32), jax.random.fold_in(key_of[4], 1), 0, 1),
        "block_funcs": touch_ends(jax.random.randint(key_of[5], (NB,), 3 * BS // 4, BS + 1), jax.random.fold_in(key_of[5], 1), 3 * BS // 4, BS).astype(jnp.int32),
    }


def mask_density(columns, funcs_all, first_col, slab_len):
    count = columns.shape[0]
    block_width = columns.shape[2]
    col_index = first_col + jnp.arange(count, dtype=jnp.int32)
    row_index = col_index[:, None] + jnp.arange(3, dtype=jnp.int32)[None, :] - 1
    col_live = (col_index >= 0) & (col_index < slab_len)
    row_live = (row_index >= 0) & (row_index < slab_len)
    col_funcs = jnp.where(col_live, funcs_all[jnp.clip(col_index, 0, slab_len - 1)], 0)
    row_funcs = jnp.where(row_live, funcs_all[jnp.clip(row_index, 0, slab_len - 1)], 0)
    lane_index = jnp.arange(block_width, dtype=jnp.int32)
    row_mask = lane_index[None, None, :] < row_funcs[:, :, None]
    col_mask = lane_index[None, :] < col_funcs[:, None]
    keep_mask = row_mask[:, :, :, None] & col_mask[:, None, None, :]
    return jnp.where(keep_mask, columns, jnp.zeros_like(columns))


def pair_valid(col_index, kept_bonds, slab_len):
    row_index = col_index[:, None] + jnp.arange(3, dtype=jnp.int32)[None, :] - 1
    row_live = (row_index >= 0) & (row_index < slab_len)
    bond_index = jnp.clip(jnp.minimum(row_index, col_index[:, None]), 0, slab_len - 1)
    bond_kept = kept_bonds[bond_index] == 1
    middle = (jnp.arange(3, dtype=jnp.int32) == 1)[None, :]
    return row_live & (middle | bond_kept)


def images_from(density, blocks):
    return jnp.einsum("kml,kmpn->lpn", density.astype(jnp.float32), blocks.astype(jnp.float32))


def reference(tensor_blocks, occupied, virtual, slot_block, pair_kept, block_funcs):
    slab_len = block_funcs.shape[0]
    region = slot_block.shape[1]
    block_width = tensor_blocks.shape[2]
    aux_width = tensor_blocks.shape[3]
    columns = jnp.arange(slab_len, dtype=jnp.int32)
    column_of_slot = (columns // region) * region + slot_block.reshape(-1).astype(jnp.int32)
    slot_of = jnp.zeros((slab_len,), jnp.int32).at[column_of_slot].set(columns)
    pair_ok = pair_valid(columns, pair_kept, slab_len)
    occ_masked = mask_density(occupied, block_funcs, 0, slab_len)
    virt_masked = mask_density(virtual, block_funcs, 0, slab_len)
    edge_zero = jnp.zeros((1,) + occ_masked.shape[1:], occ_masked.dtype)
    occ_ext = jnp.concatenate([edge_zero, occ_masked, edge_zero], axis=0)
    virt_ext = jnp.concatenate([edge_zero, virt_masked, edge_zero], axis=0)

    def tensor_block(column, entry):
        inside = (column >= 0) & (column < slab_len)
        clipped = jnp.clip(column, 0, slab_len - 1)
        blocks = tensor_blocks[slot_of[clipped], entry]
        usable = inside & pair_ok[clipped, entry]
        return jnp.where(usable, blocks, jnp.zeros_like(blocks))

    def half_column(column):
        own_blocks = jnp.stack([tensor_block(column, entry) for entry in range(3)])
        nearby = lax.dynamic_slice_in_dim(occ_ext, column, 3, 0)
        first_img = images_from(nearby[0, 1:3], own_blocks[0:2])
        middle_img = images_from(nearby[1], own_blocks)
        last_img = images_from(nearby[2, 0:2], own_blocks[1:3])
        return jnp.stack([first_img, middle_img, last_img]).astype(jnp.bfloat16)

    halves = lax.map(half_column, columns)

    def polar_rows(row_col):
        accum = jnp.zeros((3, 5, aux_width, aux_width), jnp.float32)
        for col_shift in range(3):
            partner = row_col + col_shift - 1
            inside = (partner >= 0) & (partner < slab_len)
            clipped = jnp.clip(partner, 0, slab_len - 1)
            half_blk = jnp.where(inside, halves[clipped, 2 - col_shift], 0).astype(jnp.float32)
            virt_column = lax.dynamic_index_in_dim(virt_ext, row_col + col_shift, 0, keepdims=False)
            for row_shift in range(3):
                if abs(row_shift - col_shift) > 1:
                    continue
                tensor_blk = tensor_block(row_col + row_shift - 1, 2 - row_shift).astype(jnp.float32)
                virt_blk = virt_column[row_shift - col_shift + 1].astype(jnp.float32)
                virt_image = jnp.einsum("rbs,sn->rbn", tensor_blk, virt_blk).astype(jnp.bfloat16)
                virt_image = lax.optimization_barrier(virt_image).astype(jnp.float32)
                contrib = jnp.einsum("ran,rbn->ab", half_blk, virt_image)
                accum = accum.at[col_shift, row_shift - col_shift + 2].add(contrib)
        return accum

    per_row = lax.map(polar_rows, columns)
    zero_pad = ((0, 0),) * 3
    polar = jnp.pad(per_row[:, 0], ((0, 2),) + zero_pad)
    polar = polar + jnp.pad(per_row[:, 1], ((1, 1),) + zero_pad)
    polar = polar + jnp.pad(per_row[:, 2], ((2, 0),) + zero_pad)
    return polar[1:slab_len + 1] / block_width
```

```python
import jax
import jax.numpy as jnp
from jax import lax
from jax.experimental import pallas as pl
from jax.experimental.pallas import tpu as pltpu
from jax.sharding import PartitionSpec as P

MESH = pl.DeviceIdType.MESH
BF = jnp.bfloat16
F32 = jnp.float32
SIDE = 4

NEAR = [(dx, dy) for dy in (-1, 0, 1) for dx in (-1, 0, 1) if (dx, dy) != (0, 0)]
FAR = [(2, 0), (0, 2), (2, 1), (2, -1), (1, 2), (-1, 2), (2, 2)]
RELAY = []
for _dx, _dy in FAR:
    for _half, _sign in enumerate((1, -1)):
        _first = (_sign if _dx == 2 else _dx, _sign if _dy == 2 else _dy)
        RELAY.append((_first, (_dx - _first[0], _dy - _first[1]), _half))
ALL = NEAR + FAR


def place(dx, dy):
    me = lax.axis_index("tp")
    x = lax.rem(lax.rem(me, SIDE) + (dx + SIDE), SIDE)
    y = lax.rem(me // SIDE + (dy + SIDE), SIDE)
    return y * SIDE + x


def slice_of(tp):
    x, y = lax.rem(tp, SIDE), tp // SIDE
    return y * 2 + x // 2, lax.rem(x + y, 2)


def lanes(x):
    return jnp.concatenate([x[i] for i in range(x.shape[0])], axis=1)


def dot_nt(a, b):
    return lax.dot_general(a, b, (((1,), (1,)), ((), ())), preferred_element_type=F32)


def kernel(
    inv, kt, ot, vd, vv, out,
    kh, k32, h32, r01, r2, rb, zd, zu, ed, eu, es, pt, fin, dg, acc,
    near_s, near_r, one_s, one_r, two_s, two_r, edge_s, edge_r, fin_s, fin_r, dg_s, dg_r, loc,
):
    me = lax.axis_index("tp")
    grp = lax.axis_index("grp")
    regions = lax.axis_size("grp")
    rows = 16
    kind = slice_of(me)[1]

    def dev(dx, dy):
        return (grp, place(dx, dy))

    def grp_at(step):
        return (lax.rem(grp + step + regions, regions), me)

    load = pltpu.make_async_copy(kt, kh.at[pl.ds(0, 3)], loc.at[3])
    load.start()

    barrier = pltpu.get_barrier_semaphore()
    for dx, dy in ALL:
        pl.semaphore_signal(barrier, inc=1, device_id=dev(dx, dy), device_id_type=MESH)
    for step in (1, -1):
        pl.semaphore_signal(barrier, inc=1, device_id=grp_at(step), device_id_type=MESH)
    pl.semaphore_wait(barrier, len(ALL) + 2)

    def landing(slot, origin):
        return r2.at[origin] if slot == 2 else r01.at[slot, origin]

    def source(slot, target, start, count):
        u, v = slice_of(target)
        part = pl.ds(u * rows + start, count)
        if slot == 0:
            return kt.at[v, part]
        which = 2 + 3 * v if slot == 1 else 4 - v
        return kh.at[which, part]

    copies = []

    def send(slot):
        firsts = []
        for i, (first, second, half) in enumerate(RELAY):
            target = place(first[0] + second[0], first[1] + second[1])
            c = pltpu.make_async_remote_copy(
                src_ref=source(slot, target, half * 8, 8),
                dst_ref=rb.at[slot, i],
                send_sem=one_s.at[slot, i],
                recv_sem=one_r.at[slot, i],
                device_id=dev(*first),
                device_id_type=MESH,
            )
            c.start()
            firsts.append(c)
        nears = []
        for i, (dx, dy) in enumerate(NEAR):
            c = pltpu.make_async_remote_copy(
                src_ref=source(slot, place(dx, dy), 0, rows),
                dst_ref=landing(slot, me),
                send_sem=near_s.at[slot, i],
                recv_sem=near_r.at[slot, i],
                device_id=dev(dx, dy),
                device_id_type=MESH,
            )
            c.start()
            nears.append(c)
        own = pltpu.make_async_copy(source(slot, me, 0, rows), landing(slot, me), loc.at[slot])
        own.start()
        return firsts, nears, own

    def forward(slot, firsts):
        seconds = []
        for i, (first, second, half) in enumerate(RELAY):
            firsts[i].wait_recv()
            c = pltpu.make_async_remote_copy(
                src_ref=rb.at[slot, i],
                dst_ref=landing(slot, place(-first[0], -first[1])).at[pl.ds(half * 8, 8)],
                send_sem=two_s.at[slot, i],
                recv_sem=two_r.at[slot, i],
                device_id=dev(*second),
                device_id_type=MESH,
            )
            c.start()
            seconds.append(c)
        return seconds

    def arrive(nears, own, seconds):
        own.wait()
        for c in nears + seconds:
            c.wait_recv()

    firsts0, nears0, own0 = send(0)
    load.wait()

    def half_chunk(i, _):
        cut = pl.ds(pl.multiple_of(i * 16, 16), 16)
        for d in range(3):
            k32[pl.ds(d * 2048, 2048), :] = kh[d, :, cut, :].reshape(2048, 128).astype(F32)
        for q in range(0, 16, 2):
            two = [k32[pl.ds(q + s, 384, stride=16), :] for s in range(2)]
            res = jnp.dot(
                ot[...], jnp.concatenate(two, axis=1).astype(BF), preferred_element_type=F32
            )
            for s in range(2):
                h32[pl.ds(q + s, 384, stride=16), :] = res[:, s * 128 : (s + 1) * 128]
        for e in range(3):
            kh[3 + e, :, cut, :] = h32[pl.ds(e * 2048, 2048), :].reshape(128, 16, 128).astype(BF)
        return 0

    lax.fori_loop(0, 4, half_chunk, 0)

    firsts1, nears1, own1 = send(1)
    seconds0 = forward(0, firsts0)
    firsts2, nears2, own2 = send(2)

    acc[...] = jnp.zeros_like(acc)

    def own_part(i, _):
        e, cut = i // 8, pl.ds(lax.rem(i, 8) * 16, 16)
        z = jnp.dot(kh[e, cut].reshape(1024, 128), vd[e], preferred_element_type=F32)
        acc[...] += dot_nt(lanes(kh[3 + e, cut]), lanes(z.astype(BF).reshape(16, 64, 128)))
        return 0

    seconds1 = forward(1, firsts1)
    lax.fori_loop(0, 24, own_part, 0)
    dg[me] = jnp.concatenate([acc[:32], acc[32:]], axis=1)
    shares = []
    for i, (dx, dy) in enumerate(ALL):
        c = pltpu.make_async_remote_copy(
            src_ref=dg.at[me],
            dst_ref=dg.at[me],
            send_sem=dg_s.at[i],
            recv_sem=dg_r.at[i],
            device_id=dev(dx, dy),
            device_id_type=MESH,
        )
        c.start()
        shares.append(c)

    seconds2 = forward(2, firsts2)

    arrive(nears0, own0, seconds0)
    arrive(nears1, own1, seconds1)

    es[0] = r01[0, inv[0]]
    es[1] = r01[1 - kind, inv[15]]
    edges = []
    for i, (step, dst) in enumerate(((-1, ed), (1, eu))):
        c = pltpu.make_async_remote_copy(
            src_ref=es.at[i],
            dst_ref=dst,
            send_sem=edge_s.at[i],
            recv_sem=edge_r.at[i],
            device_id=grp_at(step),
            device_id_type=MESH,
        )
        c.start()
        edges.append(c)

    def times(block, v):
        z = jnp.dot(block.reshape(1024, 128), v, preferred_element_type=F32)
        return z.astype(BF).reshape(16, 64, 128)

    def other_part(j, _):
        zd[j] = times(r01[0, inv[j + 1]], vv[j, 1])
        zu[j + 1] = times(r01[1 - kind, inv[j]], vv[j + 1, 0])
        return 0

    lax.fori_loop(0, 15, other_part, 0)
    for c in edges:
        c.wait_recv()
    zd[15] = times(ed[...], vv[15, 1])
    zu[0] = times(eu[...], vv[0, 0])

    arrive(nears2, own2, seconds2)

    @pl.when(kind == 0)
    def _():
        def part(j, _):
            half = lanes(r2[inv[j]])
            pt[j] = jnp.concatenate([dot_nt(half, lanes(zu[j])), dot_nt(half, lanes(zd[j]))], axis=1)
            return 0

        lax.fori_loop(0, 16, part, 0)

    @pl.when(kind == 1)
    def _():
        def part(j, _):
            pt[j] = jnp.concatenate(
                [
                    dot_nt(lanes(r2[inv[j]]), lanes(zu[j])),
                    dot_nt(lanes(r01[1, inv[j]]), lanes(zd[j])),
                ],
                axis=1,
            )
            return 0

        lax.fori_loop(0, 16, part, 0)

    sums = []
    for i, (dx, dy) in enumerate(ALL):
        c = pltpu.make_async_remote_copy(
            src_ref=pt.at[place(dx, dy)],
            dst_ref=fin.at[me],
            send_sem=fin_s.at[i],
            recv_sem=fin_r.at[i],
            device_id=dev(dx, dy),
            device_id_type=MESH,
        )
        c.start()
        sums.append(c)
    fin[me] = pt[me]
    for c in shares + sums:
        c.wait_recv()
    scale = 1.0 / 128
    total = fin[0]
    for k in range(1, 16):
        total = total + fin[k]
    total = total * scale
    mid = dg[inv[me]] * scale
    out[0] = jnp.zeros((64, 64), F32)
    out[1] = total[:, :64]
    out[2] = jnp.concatenate([mid[:, :64], mid[:, 64:]], axis=0)
    out[3] = total[:, 64:]
    out[4] = jnp.zeros((64, 64), F32)

    for c in firsts0 + firsts1 + firsts2 + nears0 + nears1 + nears2:
        c.wait_send()
    for c in seconds0 + seconds1 + seconds2 + edges + shares + sums:
        c.wait_send()


def fused(inv, kt, ot, vd, vv):
    dma = pltpu.SemaphoreType.DMA
    vmem = pl.BlockSpec(memory_space=pltpu.VMEM)
    near, far, every = len(NEAR), len(RELAY), len(ALL)
    return pl.pallas_call(
        kernel,
        out_shape=jax.ShapeDtypeStruct((5, 64, 64), F32),
        in_specs=[
            pl.BlockSpec(memory_space=pltpu.SMEM),
            pl.BlockSpec(memory_space=pl.ANY),
            vmem,
            vmem,
            vmem,
        ],
        out_specs=vmem,
        scratch_shapes=[
            pltpu.VMEM((6, 128, 64, 128), BF),
            pltpu.VMEM((6144, 128), F32),
            pltpu.VMEM((6144, 128), F32),
            pltpu.VMEM((2, 16, 16, 64, 128), BF),
            pltpu.VMEM((16, 16, 64, 128), BF),
            pltpu.VMEM((3, far, 8, 64, 128), BF),
            pltpu.VMEM((16, 16, 64, 128), BF),
            pltpu.VMEM((16, 16, 64, 128), BF),
            pltpu.VMEM((16, 64, 128), BF),
            pltpu.VMEM((16, 64, 128), BF),
            pltpu.VMEM((2, 16, 64, 128), BF),
            pltpu.VMEM((16, 64, 128), F32),
            pltpu.VMEM((16, 64, 128), F32),
            pltpu.VMEM((16, 32, 128), F32),
            pltpu.VMEM((64, 64), F32),
            dma((3, near)),
            dma((3, near)),
            dma((3, far)),
            dma((3, far)),
            dma((3, far)),
            dma((3, far)),
            dma((2,)),
            dma((2,)),
            dma((every,)),
            dma((every,)),
            dma((every,)),
            dma((every,)),
            dma((4,)),
        ],
        compiler_params=pltpu.CompilerParams(
            collective_id=0, has_side_effects=True, vmem_limit_bytes=60 << 20
        ),
    )(inv, kt, ot, vd, vv)


def body(tensor_blocks, occupied, virtual, slot_block, pair_kept, block_funcs):
    slab = block_funcs.shape[0]
    region = occupied.shape[0]
    width = occupied.shape[2]
    grp, tp = lax.axis_index("grp"), lax.axis_index("tp")
    regions = lax.axis_size("grp")
    first = grp * region
    slot_cols = slot_block[0]
    index = jnp.arange(region, dtype=jnp.int32)
    inv = jnp.sum(jnp.where(slot_cols[None, :] == index[:, None], index[None, :], 0), axis=1)
    local = jnp.sum(jnp.where(index == tp, slot_cols, 0))
    col = first + local

    zeros2 = jnp.zeros((2,), jnp.int32)
    funcs = lax.dynamic_slice_in_dim(
        jnp.concatenate([zeros2, block_funcs, zeros2]), first, region + 4
    )
    kept = lax.dynamic_slice_in_dim(
        jnp.concatenate([zeros2, pair_kept, zeros2]), first, region + 4
    )
    lane = jnp.arange(width, dtype=jnp.int32)

    up = [(i, i + 1) for i in range(regions - 1)]
    down = [(b, a) for a, b in up]
    low = lax.ppermute(occupied[region - 1, 1:3], "grp", up)
    high = lax.ppermute(occupied[0, 0:2], "grp", down)
    before = lax.dynamic_index_in_dim(occupied, jnp.maximum(local - 1, 0), 0, keepdims=False)
    here = lax.dynamic_index_in_dim(occupied, local, 0, keepdims=False)
    after = lax.dynamic_index_in_dim(occupied, jnp.minimum(local + 1, region - 1), 0, keepdims=False)
    before = jnp.where(local == 0, low, before[1:3])
    after = jnp.where(local == region - 1, high, after[0:2])
    none = jnp.zeros((1, width, width), occupied.dtype)
    blocks = jnp.stack(
        [
            jnp.concatenate([before, none]),
            here,
            jnp.concatenate([none, after]),
        ]
    )
    around = lax.dynamic_slice_in_dim(funcs, local + 1, 3)
    bonds = lax.dynamic_slice_in_dim(kept, local + 1, 2)
    pair_ok = jnp.stack([bonds[0] == 1, jnp.bool_(True), bonds[1] == 1])
    row_ok = (lane[None, :] < around[:, None]) & pair_ok[:, None]
    col_ok = lane[None, :] < around[:, None]
    keep = col_ok[:, None, None, :] & row_ok[None, :, :, None]
    blocks = jnp.where(keep, blocks, jnp.zeros_like(blocks))
    ot = jnp.transpose(blocks, (0, 3, 1, 2)).reshape(3 * width, 3 * width)

    own = lax.dynamic_index_in_dim(virtual, local, 0, keepdims=False)[1]
    own_ok = (lane[:, None] < around[1]) & (lane[None, :] < around[1])
    vd = jnp.where(
        own_ok[None] & pair_ok[:, None, None], own[None], jnp.zeros((3, width, width), own.dtype)
    )

    plain = lax.rem(tp // SIDE + lax.rem(tp, SIDE), 2) == 1
    row_lo = jnp.where(plain | (kept[1 : region + 1] == 1), funcs[1 : region + 1], 0)
    row_hi = jnp.where(plain | (kept[2 : region + 2] == 1), funcs[3 : region + 3], 0)
    limits = jnp.stack([row_lo, row_hi], axis=1)
    pair = jnp.stack([virtual[:, 0], virtual[:, 2]], axis=1)
    live = (lane[None, None, :, None] < limits[:, :, None, None]) & (
        lane[None, None, None, :] < funcs[2 : region + 2, None, None, None]
    )
    vv = jnp.where(live, pair, jnp.zeros_like(pair))

    return fused(inv, tensor_blocks[0], ot, vd, vv)[None]


def solution(mesh):
    placed = (
        P(("grp", "tp"), None, None, None, None),
        P("grp", None, None, None),
        P("grp", None, None, None),
        P("grp", None),
        P(),
        P(),
    )
    return jax.shard_map(
        body,
        mesh=mesh,
        in_specs=placed,
        out_specs=P(("grp", "tp"), None, None, None),
        check_vma=False,
    )
```

```python
import jax
import jax.numpy as jnp
from jax import lax
from jax.experimental import pallas as pl
from jax.experimental.pallas import tpu as pltpu
from jax.sharding import PartitionSpec as P

MESH = pl.DeviceIdType.MESH
BF = jnp.bfloat16
F32 = jnp.float32
SIDE = 4

NEAR = [(dx, dy) for dy in (-1, 0, 1) for dx in (-1, 0, 1) if (dx, dy) != (0, 0)]
FAR = [(2, 0), (0, 2), (2, 1), (2, -1), (1, 2), (-1, 2), (2, 2)]
RELAY = []
for _dx, _dy in FAR:
    for _half, _sign in enumerate((1, -1)):
        _first = (_sign if _dx == 2 else _dx, _sign if _dy == 2 else _dy)
        RELAY.append((_first, (_dx - _first[0], _dy - _first[1]), _half))
ALL = NEAR + FAR
AUX = ((0, 48), (48, 16))


def place(dx, dy):
    me = lax.axis_index("tp")
    x = lax.rem(lax.rem(me, SIDE) + (dx + SIDE), SIDE)
    y = lax.rem(me // SIDE + (dy + SIDE), SIDE)
    return y * SIDE + x


def slice_of(tp):
    x, y = lax.rem(tp, SIDE), tp // SIDE
    return y * 2 + x // 2, lax.rem(x + y, 2)


def lanes(x):
    return jnp.concatenate([x[i] for i in range(x.shape[0])], axis=1)


def dot_nt(a, b):
    return lax.dot_general(a, b, (((1,), (1,)), ((), ())), preferred_element_type=F32)


def masked(block, row_limit, col_limit):
    row = lax.broadcasted_iota(jnp.int32, block.shape, 0)
    col = lax.broadcasted_iota(jnp.int32, block.shape, 1)
    return jnp.where((row < row_limit) & (col < col_limit), block.astype(F32), 0.0)


def kernel(
    slot_ref, kept_ref, funcs_ref, tensor, occupied, virtual, out,
    inv, oe, ve, ot, vd, kh, k32, h32, r01, r2a, r2b, rb, rba, rbb, zd, zu, ed, eu, es, pt, fin, dg, acc,
    near_s, near_r, one_s, one_r, two_s, two_r, edge_s, edge_r, fin_s, fin_r, dg_s, dg_r,
    halo_s, halo_r, loc,
):
    me = lax.axis_index("tp")
    grp = lax.axis_index("grp")
    regions = lax.axis_size("grp")
    rows = 16
    kind = slice_of(me)[1]

    def dev(dx, dy):
        return (grp, place(dx, dy))

    def grp_at(step):
        return (lax.rem(grp + step + regions, regions), me)

    kt = tensor.at[0]
    region = occupied.shape[0]
    slab = funcs_ref.shape[0]
    first = grp * region
    loads = [
        pltpu.make_async_copy(occupied, oe.at[pl.ds(1, region)], loc.at[5]),
        pltpu.make_async_copy(kt, kh.at[pl.ds(0, 3)], loc.at[4]),
        pltpu.make_async_copy(virtual, ve, loc.at[6]),
    ]
    for c in loads:
        c.start()

    barrier = pltpu.get_barrier_semaphore()
    for dx, dy in ALL:
        pl.semaphore_signal(barrier, inc=1, device_id=dev(dx, dy), device_id_type=MESH)
    for step in (1, -1):
        pl.semaphore_signal(barrier, inc=1, device_id=grp_at(step), device_id_type=MESH)
    pl.semaphore_wait(barrier, len(ALL) + 2)

    def landing(slot, origin):
        return (r01.at[0, origin], r01.at[1, origin], r2a.at[origin], r2b.at[origin])[slot]

    def relayed(slot, i):
        return (rb.at[0, i], rb.at[1, i], rba.at[i], rbb.at[i])[slot]

    def source(slot, target, start, count):
        u, v = slice_of(target)
        part = pl.ds(u * rows + start, count)
        if slot == 0:
            return kt.at[v, part]
        if slot == 1:
            return kh.at[2 + 3 * v, part]
        return kh.at[4 - v, part, pl.ds(*AUX[slot - 2])]

    def send_far(slot):
        firsts = []
        for i, (hop, second, half) in enumerate(RELAY):
            target = place(hop[0] + second[0], hop[1] + second[1])
            c = pltpu.make_async_remote_copy(
                src_ref=source(slot, target, half * 8, 8),
                dst_ref=relayed(slot, i),
                send_sem=one_s.at[slot, i],
                recv_sem=one_r.at[slot, i],
                device_id=dev(*hop),
                device_id_type=MESH,
            )
            c.start()
            firsts.append(c)
        return firsts

    def send_near(slot):
        nears = []
        for i, (dx, dy) in enumerate(NEAR):
            c = pltpu.make_async_remote_copy(
                src_ref=source(slot, place(dx, dy), 0, rows),
                dst_ref=landing(slot, me),
                send_sem=near_s.at[slot, i],
                recv_sem=near_r.at[slot, i],
                device_id=dev(dx, dy),
                device_id_type=MESH,
            )
            c.start()
            nears.append(c)
        own = pltpu.make_async_copy(source(slot, me, 0, rows), landing(slot, me), loc.at[slot])
        own.start()
        return nears, own

    def forward(slot, firsts):
        seconds = []
        for i, (hop, second, half) in enumerate(RELAY):
            firsts[i].wait_recv()
            c = pltpu.make_async_remote_copy(
                src_ref=relayed(slot, i),
                dst_ref=landing(slot, place(-hop[0], -hop[1])).at[pl.ds(half * 8, 8)],
                send_sem=two_s.at[slot, i],
                recv_sem=two_r.at[slot, i],
                device_id=dev(*second),
                device_id_type=MESH,
            )
            c.start()
            seconds.append(c)
        return seconds

    def arrive(nears, own, seconds):
        own.wait()
        for c in nears + seconds:
            c.wait_recv()

    firsts0 = send_far(0)
    halos = []
    for i, (step, src, dst) in enumerate(
        (
            (1, occupied.at[region - 1, pl.ds(1, 2)], oe.at[0, pl.ds(1, 2)]),
            (-1, occupied.at[0, pl.ds(0, 2)], oe.at[region + 1, pl.ds(0, 2)]),
        )
    ):
        c = pltpu.make_async_remote_copy(
            src_ref=src,
            dst_ref=dst,
            send_sem=halo_s.at[i],
            recv_sem=halo_r.at[i],
            device_id=grp_at(step),
            device_id_type=MESH,
        )
        c.start()
        halos.append(c)
    oe[0, 0] = jnp.zeros(oe.shape[2:], BF)
    oe[region + 1, 2] = jnp.zeros(oe.shape[2:], BF)

    def funcs(col):
        inside = (col >= 0) & (col < slab)
        return jnp.where(inside, funcs_ref[jnp.clip(col, 0, slab - 1)], 0)

    def bond(col):
        inside = (col >= 0) & (col < slab)
        return jnp.where(inside, kept_ref[jnp.clip(col, 0, slab - 1)], 0)

    def find(j, _):
        at = 0
        for k in range(region):
            at = jnp.where(slot_ref[0, k] == j, k, at)
        inv[j] = at
        return 0

    lax.fori_loop(0, region, find, 0)
    local = slot_ref[0, me]
    own_col = first + local
    around = [funcs(own_col - 1), funcs(own_col), funcs(own_col + 1)]
    rows_ok = [
        jnp.where(bond(own_col - 1) == 1, around[0], 0),
        around[1],
        jnp.where(bond(own_col) == 1, around[2], 0),
    ]
    loads[0].wait()
    for c in halos:
        c.wait_recv()
    for e in range(3):
        for d in range(3):
            if abs(d - e) > 1:
                block = jnp.zeros((128, 128), BF)
            else:
                block = masked(oe[local + e, d - e + 1], rows_ok[d], around[e]).T.astype(BF)
            ot[e * 128 : (e + 1) * 128, d * 128 : (d + 1) * 128] = block
    loads[1].wait()

    def half_chunk(i, _):
        cut = pl.ds(pl.multiple_of(i * 16, 16), 16)
        for d in range(3):
            k32[pl.ds(d * 2048, 2048), :] = kh[d, :, cut, :].reshape(2048, 128).astype(F32)
        for q in range(0, 16, 2):
            two = [k32[pl.ds(q + s, 384, stride=16), :] for s in range(2)]
            res = jnp.dot(
                ot[...], jnp.concatenate(two, axis=1).astype(BF), preferred_element_type=F32
            )
            for s in range(2):
                h32[pl.ds(q + s, 384, stride=16), :] = res[:, s * 128 : (s + 1) * 128]
        for e in range(3):
            kh[3 + e, :, cut, :] = h32[pl.ds(e * 2048, 2048), :].reshape(128, 16, 128).astype(BF)
        return 0

    lax.fori_loop(0, 4, half_chunk, 0)

    firsts1 = send_far(1)
    firsts2 = send_far(2)
    firsts3 = send_far(3)
    seconds0 = forward(0, firsts0)
    seconds1 = forward(1, firsts1)
    nears0, own0 = send_near(0)
    nears1, own1 = send_near(1)
    seconds2 = forward(2, firsts2)
    nears2, own2 = send_near(2)
    seconds3 = forward(3, firsts3)
    nears3, own3 = send_near(3)
    loads[2].wait()
    for e in range(3):
        allowed = jnp.where(rows_ok[e] > 0, around[1], 0)
        vd[e] = masked(ve[local, 1], allowed, around[1]).astype(BF)
    acc[...] = jnp.zeros_like(acc)

    def own_part(i, _):
        e, cut = i // 8, pl.ds(lax.rem(i, 8) * 16, 16)
        z = jnp.dot(kh[e, cut].reshape(1024, 128), vd[e], preferred_element_type=F32)
        acc[...] += dot_nt(lanes(kh[3 + e, cut]), lanes(z.astype(BF).reshape(16, 64, 128)))
        return 0

    lax.fori_loop(0, 24, own_part, 0)
    dg[me] = jnp.concatenate([acc[:32], acc[32:]], axis=1)
    shares = []
    for i, (dx, dy) in enumerate(ALL):
        c = pltpu.make_async_remote_copy(
            src_ref=dg.at[me],
            dst_ref=dg.at[me],
            send_sem=dg_s.at[i],
            recv_sem=dg_r.at[i],
            device_id=dev(dx, dy),
            device_id_type=MESH,
        )
        c.start()
        shares.append(c)
    arrive(nears0, own0, seconds0)
    arrive(nears1, own1, seconds1)

    es[0] = r01[0, inv[0]]
    es[1] = r01[1 - kind, inv[15]]
    edges = []
    for i, (step, dst) in enumerate(((-1, ed), (1, eu))):
        c = pltpu.make_async_remote_copy(
            src_ref=es.at[i],
            dst_ref=dst,
            send_sem=edge_s.at[i],
            recv_sem=edge_r.at[i],
            device_id=grp_at(step),
            device_id_type=MESH,
        )
        c.start()
        edges.append(c)

    def times(block, j, side):
        col = first + j
        beside = funcs(col + side - 1)
        allowed = jnp.where((kind == 1) | (bond(col + side // 2 - 1) == 1), beside, 0)
        v = masked(ve[j, side], allowed, funcs(col)).astype(BF)
        z = jnp.dot(block.reshape(1024, 128), v, preferred_element_type=F32)
        return z.astype(BF).reshape(16, 64, 128)

    def other_part(j, _):
        zd[j] = times(r01[0, inv[j + 1]], j, 2)
        zu[j + 1] = times(r01[1 - kind, inv[j]], j + 1, 0)
        return 0

    lax.fori_loop(0, 15, other_part, 0)
    for c in edges:
        c.wait_recv()
    zd[15] = times(ed[...], 15, 2)
    zu[0] = times(eu[...], 0, 0)

    sums = []

    def finish(part, landed):
        start, count = AUX[part]
        cut = pl.ds(start, count)

        @pl.when(kind == 0)
        def _():
            def column(j, _):
                half = lanes(landed[inv[j]])
                pt[j, cut] = jnp.concatenate(
                    [dot_nt(half, lanes(zu[j])), dot_nt(half, lanes(zd[j]))], axis=1
                )
                return 0

            lax.fori_loop(0, 16, column, 0)

        @pl.when(kind == 1)
        def _():
            def column(j, _):
                pt[j, cut] = jnp.concatenate(
                    [
                        dot_nt(lanes(landed[inv[j]]), lanes(zu[j])),
                        dot_nt(lanes(r01[1, inv[j], :, cut]), lanes(zd[j])),
                    ],
                    axis=1,
                )
                return 0

            lax.fori_loop(0, 16, column, 0)

        for i, (dx, dy) in enumerate(ALL):
            c = pltpu.make_async_remote_copy(
                src_ref=pt.at[place(dx, dy), cut],
                dst_ref=fin.at[me, cut],
                send_sem=fin_s.at[part, i],
                recv_sem=fin_r.at[part, i],
                device_id=dev(dx, dy),
                device_id_type=MESH,
            )
            c.start()
            sums.append(c)

    arrive(nears2, own2, seconds2)
    finish(0, r2a)
    arrive(nears3, own3, seconds3)
    finish(1, r2b)
    fin[me] = pt[me]
    for c in shares + sums:
        c.wait_recv()
    scale = 1.0 / 128
    total = fin[0]
    for k in range(1, 16):
        total = total + fin[k]
    total = total * scale
    mid = dg[inv[me]] * scale
    out[0, 0] = jnp.zeros((64, 64), F32)
    out[0, 1] = total[:, :64]
    out[0, 2] = jnp.concatenate([mid[:, :64], mid[:, 64:]], axis=0)
    out[0, 3] = total[:, 64:]
    out[0, 4] = jnp.zeros((64, 64), F32)

    for c in firsts0 + firsts1 + firsts2 + firsts3 + nears0 + nears1 + nears2 + nears3:
        c.wait_send()
    for c in seconds0 + seconds1 + seconds2 + seconds3 + halos + edges + shares + sums:
        c.wait_send()


def body(tensor_blocks, occupied, virtual, slot_block, pair_kept, block_funcs):
    dma = pltpu.SemaphoreType.DMA
    smem = pl.BlockSpec(memory_space=pltpu.SMEM)
    hbm = pl.BlockSpec(memory_space=pl.ANY)
    near, far, every = len(NEAR), len(RELAY), len(ALL)
    return pl.pallas_call(
        kernel,
        out_shape=jax.ShapeDtypeStruct((1, 5, 64, 64), F32),
        in_specs=[smem, smem, smem, hbm, hbm, hbm],
        out_specs=pl.BlockSpec(memory_space=pltpu.VMEM),
        scratch_shapes=[
            pltpu.SMEM((16,), jnp.int32),
            pltpu.VMEM((18, 3, 128, 128), BF),
            pltpu.VMEM((16, 3, 128, 128), BF),
            pltpu.VMEM((384, 384), BF),
            pltpu.VMEM((3, 128, 128), BF),
            pltpu.VMEM((6, 128, 64, 128), BF),
            pltpu.VMEM((6144, 128), F32),
            pltpu.VMEM((6144, 128), F32),
            pltpu.VMEM((2, 16, 16, 64, 128), BF),
            pltpu.VMEM((16, 16, AUX[0][1], 128), BF),
            pltpu.VMEM((16, 16, AUX[1][1], 128), BF),
            pltpu.VMEM((2, far, 8, 64, 128), BF),
            pltpu.VMEM((far, 8, AUX[0][1], 128), BF),
            pltpu.VMEM((far, 8, AUX[1][1], 128), BF),
            pltpu.VMEM((16, 16, 64, 128), BF),
            pltpu.VMEM((16, 16, 64, 128), BF),
            pltpu.VMEM((16, 64, 128), BF),
            pltpu.VMEM((16, 64, 128), BF),
            pltpu.VMEM((2, 16, 64, 128), BF),
            pltpu.VMEM((16, 64, 128), F32),
            pltpu.VMEM((16, 64, 128), F32),
            pltpu.VMEM((16, 32, 128), F32),
            pltpu.VMEM((64, 64), F32),
            dma((4, near)),
            dma((4, near)),
            dma((4, far)),
            dma((4, far)),
            dma((4, far)),
            dma((4, far)),
            dma((2,)),
            dma((2,)),
            dma((2, every)),
            dma((2, every)),
            dma((every,)),
            dma((every,)),
            dma((2,)),
            dma((2,)),
            dma((7,)),
        ],
        compiler_params=pltpu.CompilerParams(
            collective_id=0, has_side_effects=True, vmem_limit_bytes=60 << 20
        ),
    )(slot_block, pair_kept, block_funcs, tensor_blocks, occupied, virtual)


def solution(mesh):
    placed = (
        P(("grp", "tp"), None, None, None, None),
        P("grp", None, None, None),
        P("grp", None, None, None),
        P("grp", None),
        P(),
        P(),
    )
    return jax.shard_map(
        body,
        mesh=mesh,
        in_specs=placed,
        out_specs=P(("grp", "tp"), None, None, None),
        check_vma=False,
    )
```

```python
import jax
import jax.numpy as jnp
from jax import lax
from jax.experimental import pallas as pl
from jax.experimental.pallas import tpu as pltpu
from jax.sharding import PartitionSpec as P

MESH = pl.DeviceIdType.MESH
BF = jnp.bfloat16
F32 = jnp.float32
SIDE = 4

NEAR = [(dx, dy) for dy in (-1, 0, 1) for dx in (-1, 0, 1) if (dx, dy) != (0, 0)]
FAR = [(2, 0), (0, 2), (2, 1), (2, -1), (1, 2), (-1, 2), (2, 2)]
RELAY = []
for _dx, _dy in FAR:
    for _half, _sign in enumerate((1, -1)):
        _first = (_sign if _dx == 2 else _dx, _sign if _dy == 2 else _dy)
        RELAY.append((_first, (_dx - _first[0], _dy - _first[1]), _half))
ALL = NEAR + FAR
AUX = ((0, 48), (48, 16))


def place(dx, dy):
    me = lax.axis_index("tp")
    x = lax.rem(lax.rem(me, SIDE) + (dx + SIDE), SIDE)
    y = lax.rem(me // SIDE + (dy + SIDE), SIDE)
    return y * SIDE + x


def slice_of(tp):
    x, y = lax.rem(tp, SIDE), tp // SIDE
    return y * 2 + x // 2, lax.rem(x + y, 2)


def lanes(x):
    return jnp.concatenate([x[i] for i in range(x.shape[0])], axis=1)


def dot_nt(a, b):
    return lax.dot_general(a, b, (((1,), (1,)), ((), ())), preferred_element_type=F32)


def masked(block, row_limit, col_limit):
    row = lax.broadcasted_iota(jnp.int32, block.shape, 0)
    col = lax.broadcasted_iota(jnp.int32, block.shape, 1)
    return jnp.where((row < row_limit) & (col < col_limit), block.astype(F32), 0.0)


def kernel(
    slot_ref, kept_ref, funcs_ref, tensor, occupied, virtual, out,
    inv, oe, ve, ot, vd, kh, k32, h32, r01, r2a, r2b, rb, rba, rbb, zd, zu, ed, eu, es, pt, fin, dg, acc,
    near_s, near_r, one_s, one_r, two_s, two_r, edge_s, edge_r, fin_s, fin_r, dg_s, dg_r,
    halo_s, halo_r, loc, ready,
):
    me = lax.axis_index("tp")
    grp = lax.axis_index("grp")
    regions = lax.axis_size("grp")
    rows = 16
    kind = slice_of(me)[1]

    def dev(dx, dy):
        return (grp, place(dx, dy))

    def grp_at(step):
        return (lax.rem(grp + step + regions, regions), me)

    kt = tensor.at[0]
    region = occupied.shape[0]
    slab = funcs_ref.shape[0]
    first = grp * region
    loads = [
        pltpu.make_async_copy(occupied, oe.at[pl.ds(1, region)], loc.at[5]),
        pltpu.make_async_copy(kt, kh.at[pl.ds(0, 3)], loc.at[4]),
        pltpu.make_async_copy(virtual, ve, loc.at[6]),
    ]
    for c in loads:
        c.start()

    barrier = pltpu.get_barrier_semaphore()
    for dx, dy in ALL:
        pl.semaphore_signal(barrier, inc=1, device_id=dev(dx, dy), device_id_type=MESH)
    pl.semaphore_signal(barrier, inc=1, device_id=grp_at(1), device_id_type=MESH)
    pl.semaphore_wait(barrier, len(ALL) + 1)
    pl.semaphore_signal(ready, inc=1, device_id=grp_at(-1), device_id_type=MESH)

    def landing(slot, origin):
        return (r01.at[0, origin], r01.at[1, origin], r2a.at[origin], r2b.at[origin])[slot]

    def relayed(slot, i):
        return (rb.at[0, i], rb.at[1, i], rba.at[i], rbb.at[i])[slot]

    def source(slot, target, start, count, early=False):
        u, v = slice_of(target)
        part = pl.ds(u * rows + start, count)
        if slot == 0:
            return kt.at[v, part]
        if slot == 1 and early:
            return kt.at[2, part]
        if slot == 1:
            return kh.at[2 + 3 * v, part]
        return kh.at[4 - v, part, pl.ds(*AUX[slot - 2])]

    def send_far(slot, only=None):
        firsts = []
        for i, (hop, second, half) in enumerate(RELAY):
            target = place(hop[0] + second[0], hop[1] + second[1])
            c = pltpu.make_async_remote_copy(
                src_ref=source(slot, target, half * 8, 8, only == 0),
                dst_ref=relayed(slot, i),
                send_sem=one_s.at[slot, i],
                recv_sem=one_r.at[slot, i],
                device_id=dev(*hop),
                device_id_type=MESH,
            )
            if only is None:
                c.start()
            else:
                pl.when(slice_of(target)[1] == only)(c.start)
            firsts.append(c)
        return firsts

    def send_near(slot):
        nears = []
        for i, (dx, dy) in enumerate(NEAR):
            c = pltpu.make_async_remote_copy(
                src_ref=source(slot, place(dx, dy), 0, rows),
                dst_ref=landing(slot, me),
                send_sem=near_s.at[slot, i],
                recv_sem=near_r.at[slot, i],
                device_id=dev(dx, dy),
                device_id_type=MESH,
            )
            c.start()
            nears.append(c)
        own = pltpu.make_async_copy(source(slot, me, 0, rows), landing(slot, me), loc.at[slot])
        own.start()
        return nears, own

    def forward(slot, firsts):
        seconds = []
        for i, (hop, second, half) in enumerate(RELAY):
            firsts[i].wait_recv()
            c = pltpu.make_async_remote_copy(
                src_ref=relayed(slot, i),
                dst_ref=landing(slot, place(-hop[0], -hop[1])).at[pl.ds(half * 8, 8)],
                send_sem=two_s.at[slot, i],
                recv_sem=two_r.at[slot, i],
                device_id=dev(*second),
                device_id_type=MESH,
            )
            c.start()
            seconds.append(c)
        return seconds

    def arrive(nears, own, seconds):
        own.wait()
        for c in nears + seconds:
            c.wait_recv()

    firsts0 = send_far(0)
    send_far(1, 0)
    oe[0, 0] = jnp.zeros(oe.shape[2:], BF)
    oe[region + 1, 2] = jnp.zeros(oe.shape[2:], BF)

    def funcs(col):
        inside = (col >= 0) & (col < slab)
        return jnp.where(inside, funcs_ref[jnp.clip(col, 0, slab - 1)], 0)

    def bond(col):
        inside = (col >= 0) & (col < slab)
        return jnp.where(inside, kept_ref[jnp.clip(col, 0, slab - 1)], 0)

    def find(j, _):
        at = 0
        for k in range(region):
            at = jnp.where(slot_ref[0, k] == j, k, at)
        inv[j] = at
        return 0

    lax.fori_loop(0, region, find, 0)

    halos = []
    for i, (step, src, dst) in enumerate(
        (
            (-1, occupied.at[0, pl.ds(0, 2)], oe.at[region + 1, pl.ds(0, 2)]),
            (1, occupied.at[region - 1, pl.ds(1, 2)], oe.at[0, pl.ds(1, 2)]),
        )
    ):
        if step == 1:
            pl.semaphore_wait(ready, 1)
        c = pltpu.make_async_remote_copy(
            src_ref=src,
            dst_ref=dst,
            send_sem=halo_s.at[i],
            recv_sem=halo_r.at[i],
            device_id=grp_at(step),
            device_id_type=MESH,
        )
        c.start()
        halos.append(c)

    local = slot_ref[0, me]
    own_col = first + local
    around = [funcs(own_col - 1), funcs(own_col), funcs(own_col + 1)]
    rows_ok = [
        jnp.where(bond(own_col - 1) == 1, around[0], 0),
        around[1],
        jnp.where(bond(own_col) == 1, around[2], 0),
    ]
    loads[0].wait()
    for c in halos:
        c.wait_recv()
    for e in range(3):
        for d in range(3):
            if abs(d - e) > 1:
                block = jnp.zeros((128, 128), BF)
            else:
                block = masked(oe[local + e, d - e + 1], rows_ok[d], around[e]).T.astype(BF)
            ot[e * 128 : (e + 1) * 128, d * 128 : (d + 1) * 128] = block
    loads[1].wait()

    def half_chunk(i, _):
        cut = pl.ds(pl.multiple_of(i * 16, 16), 16)
        for d in range(3):
            k32[pl.ds(d * 2048, 2048), :] = kh[d, :, cut, :].reshape(2048, 128).astype(F32)
        for q in range(0, 16, 2):
            two = [k32[pl.ds(q + s, 384, stride=16), :] for s in range(2)]
            res = jnp.dot(
                ot[...], jnp.concatenate(two, axis=1).astype(BF), preferred_element_type=F32
            )
            for s in range(2):
                h32[pl.ds(q + s, 384, stride=16), :] = res[:, s * 128 : (s + 1) * 128]
        for e in range(3):
            kh[3 + e, :, cut, :] = h32[pl.ds(e * 2048, 2048), :].reshape(128, 16, 128).astype(BF)
        return 0

    lax.fori_loop(0, 4, half_chunk, 0)

    firsts1 = send_far(1, 1)
    firsts2 = send_far(2)
    firsts3 = send_far(3)
    seconds0 = forward(0, firsts0)
    seconds1 = forward(1, firsts1)
    nears0, own0 = send_near(0)
    nears1, own1 = send_near(1)
    seconds2 = forward(2, firsts2)
    nears2, own2 = send_near(2)
    seconds3 = forward(3, firsts3)
    nears3, own3 = send_near(3)
    loads[2].wait()
    for e in range(3):
        allowed = jnp.where(rows_ok[e] > 0, around[1], 0)
        vd[e] = masked(ve[local, 1], allowed, around[1]).astype(BF)
    acc[...] = jnp.zeros_like(acc)

    def own_part(i, _):
        e, cut = i // 8, pl.ds(lax.rem(i, 8) * 16, 16)
        z = jnp.dot(kh[e, cut].reshape(1024, 128), vd[e], preferred_element_type=F32)
        acc[...] += dot_nt(lanes(kh[3 + e, cut]), lanes(z.astype(BF).reshape(16, 64, 128)))
        return 0

    lax.fori_loop(0, 24, own_part, 0)
    dg[me] = jnp.concatenate([acc[:32], acc[32:]], axis=1)
    shares = []
    for i, (dx, dy) in enumerate(ALL):
        c = pltpu.make_async_remote_copy(
            src_ref=dg.at[me],
            dst_ref=dg.at[me],
            send_sem=dg_s.at[i],
            recv_sem=dg_r.at[i],
            device_id=dev(dx, dy),
            device_id_type=MESH,
        )
        c.start()
        shares.append(c)
    arrive(nears0, own0, seconds0)
    arrive(nears1, own1, seconds1)

    es[0] = r01[0, inv[0]]
    es[1] = r01[1 - kind, inv[15]]
    edges = []
    for i, (step, dst) in enumerate(((-1, ed), (1, eu))):
        c = pltpu.make_async_remote_copy(
            src_ref=es.at[i],
            dst_ref=dst,
            send_sem=edge_s.at[i],
            recv_sem=edge_r.at[i],
            device_id=grp_at(step),
            device_id_type=MESH,
        )
        c.start()
        edges.append(c)

    def times(block, j, side):
        col = first + j
        beside = funcs(col + side - 1)
        allowed = jnp.where((kind == 1) | (bond(col + side // 2 - 1) == 1), beside, 0)
        v = masked(ve[j, side], allowed, funcs(col)).astype(BF)
        z = jnp.dot(block.reshape(1024, 128), v, preferred_element_type=F32)
        return z.astype(BF).reshape(16, 64, 128)

    def other_part(j, _):
        zd[j] = times(r01[0, inv[j + 1]], j, 2)
        zu[j + 1] = times(r01[1 - kind, inv[j]], j + 1, 0)
        return 0

    lax.fori_loop(0, 15, other_part, 0)
    for c in edges:
        c.wait_recv()
    zd[15] = times(ed[...], 15, 2)
    zu[0] = times(eu[...], 0, 0)

    sums = []

    def finish(part, landed):
        start, count = AUX[part]
        cut = pl.ds(start, count)

        @pl.when(kind == 0)
        def _():
            def column(j, _):
                half = lanes(landed[inv[j]])
                pt[j, cut] = jnp.concatenate(
                    [dot_nt(half, lanes(zu[j])), dot_nt(half, lanes(zd[j]))], axis=1
                )
                return 0

            lax.fori_loop(0, 16, column, 0)

        @pl.when(kind == 1)
        def _():
            def column(j, _):
                pt[j, cut] = jnp.concatenate(
                    [
                        dot_nt(lanes(landed[inv[j]]), lanes(zu[j])),
                        dot_nt(lanes(r01[1, inv[j], :, cut]), lanes(zd[j])),
                    ],
                    axis=1,
                )
                return 0

            lax.fori_loop(0, 16, column, 0)

        for i, (dx, dy) in enumerate(ALL):
            c = pltpu.make_async_remote_copy(
                src_ref=pt.at[place(dx, dy), cut],
                dst_ref=fin.at[me, cut],
                send_sem=fin_s.at[part, i],
                recv_sem=fin_r.at[part, i],
                device_id=dev(dx, dy),
                device_id_type=MESH,
            )
            c.start()
            sums.append(c)

    arrive(nears2, own2, seconds2)
    finish(0, r2a)
    arrive(nears3, own3, seconds3)
    finish(1, r2b)
    fin[me] = pt[me]
    for c in shares + sums:
        c.wait_recv()
    scale = 1.0 / 128
    total = fin[0]
    for k in range(1, 16):
        total = total + fin[k]
    total = total * scale
    mid = dg[inv[me]] * scale
    out[0, 0] = jnp.zeros((64, 64), F32)
    out[0, 1] = total[:, :64]
    out[0, 2] = jnp.concatenate([mid[:, :64], mid[:, 64:]], axis=0)
    out[0, 3] = total[:, 64:]
    out[0, 4] = jnp.zeros((64, 64), F32)

    for c in firsts0 + firsts1 + firsts2 + firsts3 + nears0 + nears1 + nears2 + nears3:
        c.wait_send()
    for c in seconds0 + seconds1 + seconds2 + seconds3 + halos + edges + shares + sums:
        c.wait_send()


def body(tensor_blocks, occupied, virtual, slot_block, pair_kept, block_funcs):
    dma = pltpu.SemaphoreType.DMA
    smem = pl.BlockSpec(memory_space=pltpu.SMEM)
    hbm = pl.BlockSpec(memory_space=pl.ANY)
    near, far, every = len(NEAR), len(RELAY), len(ALL)
    return pl.pallas_call(
        kernel,
        out_shape=jax.ShapeDtypeStruct((1, 5, 64, 64), F32),
        in_specs=[smem, smem, smem, hbm, hbm, hbm],
        out_specs=pl.BlockSpec(memory_space=pltpu.VMEM),
        scratch_shapes=[
            pltpu.SMEM((16,), jnp.int32),
            pltpu.VMEM((18, 3, 128, 128), BF),
            pltpu.VMEM((16, 3, 128, 128), BF),
            pltpu.VMEM((384, 384), BF),
            pltpu.VMEM((3, 128, 128), BF),
            pltpu.VMEM((6, 128, 64, 128), BF),
            pltpu.VMEM((6144, 128), F32),
            pltpu.VMEM((6144, 128), F32),
            pltpu.VMEM((2, 16, 16, 64, 128), BF),
            pltpu.VMEM((16, 16, AUX[0][1], 128), BF),
            pltpu.VMEM((16, 16, AUX[1][1], 128), BF),
            pltpu.VMEM((2, far, 8, 64, 128), BF),
            pltpu.VMEM((far, 8, AUX[0][1], 128), BF),
            pltpu.VMEM((far, 8, AUX[1][1], 128), BF),
            pltpu.VMEM((16, 16, 64, 128), BF),
            pltpu.VMEM((16, 16, 64, 128), BF),
            pltpu.VMEM((16, 64, 128), BF),
            pltpu.VMEM((16, 64, 128), BF),
            pltpu.VMEM((2, 16, 64, 128), BF),
            pltpu.VMEM((16, 64, 128), F32),
            pltpu.VMEM((16, 64, 128), F32),
            pltpu.VMEM((16, 32, 128), F32),
            pltpu.VMEM((64, 64), F32),
            dma((4, near)),
            dma((4, near)),
            dma((4, far)),
            dma((4, far)),
            dma((4, far)),
            dma((4, far)),
            dma((2,)),
            dma((2,)),
            dma((2, every)),
            dma((2, every)),
            dma((every,)),
            dma((every,)),
            dma((2,)),
            dma((2,)),
            dma((7,)),
            pltpu.SemaphoreType.REGULAR,
        ],
        compiler_params=pltpu.CompilerParams(
            collective_id=0, has_side_effects=True, vmem_limit_bytes=60 << 20
        ),
    )(slot_block, pair_kept, block_funcs, tensor_blocks, occupied, virtual)


def solution(mesh):
    placed = (
        P(("grp", "tp"), None, None, None, None),
        P("grp", None, None, None),
        P("grp", None, None, None),
        P("grp", None),
        P(),
        P(),
    )
    return jax.shard_map(
        body,
        mesh=mesh,
        in_specs=placed,
        out_specs=P(("grp", "tp"), None, None, None),
        check_vma=False,
    )
```

```python
import jax
import jax.numpy as jnp
from jax import lax
from jax.experimental import pallas as pl
from jax.experimental.pallas import tpu as pltpu
from jax.sharding import PartitionSpec as P

MESH = pl.DeviceIdType.MESH
BF = jnp.bfloat16
F32 = jnp.float32
SIDE = 4

NEAR = [(-1, -1), (1, -1), (-1, 1), (1, 1), (-1, 0), (1, 0), (0, -1), (0, 1)]
FAR = [(2, 0), (0, 2), (2, 1), (2, -1), (1, 2), (-1, 2), (2, 2)]
RELAY = []
for _dx, _dy in FAR:
    for _half, _sign in enumerate((1, -1)):
        _first = (_sign if _dx == 2 else _dx, _sign if _dy == 2 else _dy)
        RELAY.append((_first, (_dx - _first[0], _dy - _first[1]), _half))
ALL = NEAR + FAR
AUX = ((0, 48), (48, 16))


def place(dx, dy):
    me = lax.axis_index("tp")
    x = lax.rem(lax.rem(me, SIDE) + (dx + SIDE), SIDE)
    y = lax.rem(me // SIDE + (dy + SIDE), SIDE)
    return y * SIDE + x


def slice_of(tp):
    x, y = lax.rem(tp, SIDE), tp // SIDE
    return y * 2 + x // 2, lax.rem(x + y, 2)


def lanes(x):
    return jnp.concatenate([x[i] for i in range(x.shape[0])], axis=1)


def dot_nt(a, b):
    return lax.dot_general(a, b, (((1,), (1,)), ((), ())), preferred_element_type=F32)


def masked(block, row_limit, col_limit):
    row = lax.broadcasted_iota(jnp.int32, block.shape, 0)
    col = lax.broadcasted_iota(jnp.int32, block.shape, 1)
    return jnp.where((row < row_limit) & (col < col_limit), block.astype(F32), 0.0)


def kernel(
    slot_ref, kept_ref, funcs_ref, tensor, occupied, virtual, out,
    inv, oe, ve, ot, vd, kh, k32, h32, r01, r2a, r2b, rb, rba, rbb, zd, zu, ed, eu, es, pt, fin, dg, acc,
    near_s, near_r, one_s, one_r, two_s, two_r, edge_s, edge_r, fin_s, fin_r, dg_s, dg_r,
    halo_s, halo_r, loc, ready,
):
    me = lax.axis_index("tp")
    grp = lax.axis_index("grp")
    regions = lax.axis_size("grp")
    rows = 16
    kind = slice_of(me)[1]

    def dev(dx, dy):
        return (grp, place(dx, dy))

    def grp_at(step):
        return (lax.rem(grp + step + regions, regions), me)

    kt = tensor.at[0]
    region = occupied.shape[0]
    slab = funcs_ref.shape[0]
    first = grp * region
    loads = [
        pltpu.make_async_copy(occupied, oe.at[pl.ds(1, region)], loc.at[5]),
        pltpu.make_async_copy(kt, kh.at[pl.ds(0, 3)], loc.at[4]),
        pltpu.make_async_copy(virtual, ve, loc.at[6]),
    ]
    for c in loads:
        c.start()

    barrier = pltpu.get_barrier_semaphore()
    for dx, dy in NEAR:
        pl.semaphore_signal(barrier, inc=1, device_id=dev(dx, dy), device_id_type=MESH)
    pl.semaphore_signal(barrier, inc=1, device_id=grp_at(1), device_id_type=MESH)
    pl.semaphore_wait(barrier, len(NEAR) + 1)
    pl.semaphore_signal(ready, inc=1, device_id=grp_at(-1), device_id_type=MESH)

    def landing(slot, origin):
        return (r01.at[0, origin], r01.at[1, origin], r2a.at[origin], r2b.at[origin])[slot]

    def relayed(slot, i):
        return (rb.at[0, i], rb.at[1, i], rba.at[i], rbb.at[i])[slot]

    def source(slot, target, start, count, early=False):
        u, v = slice_of(target)
        part = pl.ds(u * rows + start, count)
        if slot == 0:
            return kt.at[v, part]
        if slot == 1 and early:
            return kt.at[2, part]
        if slot == 1:
            return kh.at[2 + 3 * v, part]
        return kh.at[4 - v, part, pl.ds(*AUX[slot - 2])]

    def send_far(slot, only=None):
        firsts = []
        for i, (hop, second, half) in enumerate(RELAY):
            target = place(hop[0] + second[0], hop[1] + second[1])
            c = pltpu.make_async_remote_copy(
                src_ref=source(slot, target, half * 8, 8, only == 0),
                dst_ref=relayed(slot, i),
                send_sem=one_s.at[slot, i],
                recv_sem=one_r.at[slot, i],
                device_id=dev(*hop),
                device_id_type=MESH,
            )
            if only is None:
                c.start()
            else:
                pl.when(slice_of(target)[1] == only)(c.start)
            firsts.append(c)
        return firsts

    def send_near(slot):
        nears = []
        for i, (dx, dy) in enumerate(NEAR):
            c = pltpu.make_async_remote_copy(
                src_ref=source(slot, place(dx, dy), 0, rows),
                dst_ref=landing(slot, me),
                send_sem=near_s.at[slot, i],
                recv_sem=near_r.at[slot, i],
                device_id=dev(dx, dy),
                device_id_type=MESH,
            )
            c.start()
            nears.append(c)
        own = pltpu.make_async_copy(source(slot, me, 0, rows), landing(slot, me), loc.at[slot])
        own.start()
        return nears, own

    def forward(slot, firsts):
        seconds = []
        for i, (hop, second, half) in enumerate(RELAY):
            firsts[i].wait_recv()
            c = pltpu.make_async_remote_copy(
                src_ref=relayed(slot, i),
                dst_ref=landing(slot, place(-hop[0], -hop[1])).at[pl.ds(half * 8, 8)],
                send_sem=two_s.at[slot, i],
                recv_sem=two_r.at[slot, i],
                device_id=dev(*second),
                device_id_type=MESH,
            )
            c.start()
            seconds.append(c)
        return seconds

    def arrive(nears, own, seconds):
        own.wait()
        for c in nears + seconds:
            c.wait_recv()

    firsts0 = send_far(0)
    send_far(1, 0)
    oe[0, 0] = jnp.zeros(oe.shape[2:], BF)
    oe[region + 1, 2] = jnp.zeros(oe.shape[2:], BF)

    def funcs(col):
        inside = (col >= 0) & (col < slab)
        return jnp.where(inside, funcs_ref[jnp.clip(col, 0, slab - 1)], 0)

    def bond(col):
        inside = (col >= 0) & (col < slab)
        return jnp.where(inside, kept_ref[jnp.clip(col, 0, slab - 1)], 0)

    def find(j, _):
        at = 0
        for k in range(region):
            at = jnp.where(slot_ref[0, k] == j, k, at)
        inv[j] = at
        return 0

    lax.fori_loop(0, region, find, 0)

    halos = []
    for i, (step, src, dst) in enumerate(
        (
            (-1, occupied.at[0, pl.ds(0, 2)], oe.at[region + 1, pl.ds(0, 2)]),
            (1, occupied.at[region - 1, pl.ds(1, 2)], oe.at[0, pl.ds(1, 2)]),
        )
    ):
        if step == 1:
            pl.semaphore_wait(ready, 1)
        c = pltpu.make_async_remote_copy(
            src_ref=src,
            dst_ref=dst,
            send_sem=halo_s.at[i],
            recv_sem=halo_r.at[i],
            device_id=grp_at(step),
            device_id_type=MESH,
        )
        c.start()
        halos.append(c)

    local = slot_ref[0, me]
    own_col = first + local
    around = [funcs(own_col - 1), funcs(own_col), funcs(own_col + 1)]
    rows_ok = [
        jnp.where(bond(own_col - 1) == 1, around[0], 0),
        around[1],
        jnp.where(bond(own_col) == 1, around[2], 0),
    ]
    loads[0].wait()
    for c in halos:
        c.wait_recv()
    for e in range(3):
        for d in range(3):
            if abs(d - e) > 1:
                block = jnp.zeros((128, 128), BF)
            else:
                block = masked(oe[local + e, d - e + 1], rows_ok[d], around[e]).T.astype(BF)
            ot[e * 128 : (e + 1) * 128, d * 128 : (d + 1) * 128] = block
    loads[1].wait()

    def half_chunk(i, _):
        cut = pl.ds(pl.multiple_of(i * 16, 16), 16)
        for d in range(3):
            k32[pl.ds(d * 2048, 2048), :] = kh[d, :, cut, :].reshape(2048, 128).astype(F32)
        for q in range(0, 16, 2):
            two = [k32[pl.ds(q + s, 384, stride=16), :] for s in range(2)]
            res = jnp.dot(
                ot[...], jnp.concatenate(two, axis=1).astype(BF), preferred_element_type=F32
            )
            for s in range(2):
                h32[pl.ds(q + s, 384, stride=16), :] = res[:, s * 128 : (s + 1) * 128]
        for e in range(3):
            kh[3 + e, :, cut, :] = h32[pl.ds(e * 2048, 2048), :].reshape(128, 16, 128).astype(BF)
        return 0

    lax.fori_loop(0, 4, half_chunk, 0)

    firsts1 = send_far(1, 1)
    firsts2 = send_far(2)
    firsts3 = send_far(3)
    seconds0 = forward(0, firsts0)
    seconds1 = forward(1, firsts1)
    nears0, own0 = send_near(0)
    nears1, own1 = send_near(1)
    seconds2 = forward(2, firsts2)
    nears2, own2 = send_near(2)
    seconds3 = forward(3, firsts3)
    nears3, own3 = send_near(3)
    loads[2].wait()
    for e in range(3):
        allowed = jnp.where(rows_ok[e] > 0, around[1], 0)
        vd[e] = masked(ve[local, 1], allowed, around[1]).astype(BF)
    acc[...] = jnp.zeros_like(acc)

    def own_part(i, _):
        e, cut = i // 8, pl.ds(lax.rem(i, 8) * 16, 16)
        z = jnp.dot(kh[e, cut].reshape(1024, 128), vd[e], preferred_element_type=F32)
        acc[...] += dot_nt(lanes(kh[3 + e, cut]), lanes(z.astype(BF).reshape(16, 64, 128)))
        return 0

    lax.fori_loop(0, 24, own_part, 0)
    dg[me] = jnp.concatenate([acc[:32], acc[32:]], axis=1)
    arrive(nears0, own0, seconds0)
    arrive(nears1, own1, seconds1)

    shares = []
    for i, (dx, dy) in enumerate(ALL):
        c = pltpu.make_async_remote_copy(
            src_ref=dg.at[me],
            dst_ref=dg.at[me],
            send_sem=dg_s.at[i],
            recv_sem=dg_r.at[i],
            device_id=dev(dx, dy),
            device_id_type=MESH,
        )
        c.start()
        shares.append(c)

    es[0] = r01[0, inv[0]]
    es[1] = r01[1 - kind, inv[15]]
    edges = []
    for i, (step, dst) in enumerate(((-1, ed), (1, eu))):
        c = pltpu.make_async_remote_copy(
            src_ref=es.at[i],
            dst_ref=dst,
            send_sem=edge_s.at[i],
            recv_sem=edge_r.at[i],
            device_id=grp_at(step),
            device_id_type=MESH,
        )
        c.start()
        edges.append(c)

    def times(block, j, side):
        col = first + j
        beside = funcs(col + side - 1)
        allowed = jnp.where((kind == 1) | (bond(col + side // 2 - 1) == 1), beside, 0)
        v = masked(ve[j, side], allowed, funcs(col)).astype(BF)
        z = jnp.dot(block.reshape(1024, 128), v, preferred_element_type=F32)
        return z.astype(BF).reshape(16, 64, 128)

    def other_part(j, _):
        zd[j] = times(r01[0, inv[j + 1]], j, 2)
        zu[j + 1] = times(r01[1 - kind, inv[j]], j + 1, 0)
        return 0

    lax.fori_loop(0, 15, other_part, 0)
    for c in edges:
        c.wait_recv()
    zd[15] = times(ed[...], 15, 2)
    zu[0] = times(eu[...], 0, 0)

    sums = []

    def finish(part, landed):
        start, count = AUX[part]
        cut = pl.ds(start, count)

        @pl.when(kind == 0)
        def _():
            def column(j, _):
                half = lanes(landed[inv[j]])
                pt[j, cut] = jnp.concatenate(
                    [dot_nt(half, lanes(zu[j])), dot_nt(half, lanes(zd[j]))], axis=1
                )
                return 0

            lax.fori_loop(0, 16, column, 0)

        @pl.when(kind == 1)
        def _():
            def column(j, _):
                pt[j, cut] = jnp.concatenate(
                    [
                        dot_nt(lanes(landed[inv[j]]), lanes(zu[j])),
                        dot_nt(lanes(r01[1, inv[j], :, cut]), lanes(zd[j])),
                    ],
                    axis=1,
                )
                return 0

            lax.fori_loop(0, 16, column, 0)

        for i, (dx, dy) in enumerate(ALL):
            c = pltpu.make_async_remote_copy(
                src_ref=pt.at[place(dx, dy), cut],
                dst_ref=fin.at[me, cut],
                send_sem=fin_s.at[part, i],
                recv_sem=fin_r.at[part, i],
                device_id=dev(dx, dy),
                device_id_type=MESH,
            )
            c.start()
            sums.append(c)

    arrive(nears2, own2, seconds2)
    finish(0, r2a)
    arrive(nears3, own3, seconds3)
    finish(1, r2b)
    fin[me] = pt[me]
    for c in shares + sums:
        c.wait_recv()
    scale = 1.0 / 128
    total = fin[0]
    for k in range(1, 16):
        total = total + fin[k]
    total = total * scale
    mid = dg[inv[me]] * scale
    out[0, 0] = jnp.zeros((64, 64), F32)
    out[0, 1] = total[:, :64]
    out[0, 2] = jnp.concatenate([mid[:, :64], mid[:, 64:]], axis=0)
    out[0, 3] = total[:, 64:]
    out[0, 4] = jnp.zeros((64, 64), F32)

    for c in firsts0 + firsts1 + firsts2 + firsts3 + nears0 + nears1 + nears2 + nears3:
        c.wait_send()
    for c in seconds0 + seconds1 + seconds2 + seconds3 + halos + edges + shares + sums:
        c.wait_send()


def body(tensor_blocks, occupied, virtual, slot_block, pair_kept, block_funcs):
    dma = pltpu.SemaphoreType.DMA
    smem = pl.BlockSpec(memory_space=pltpu.SMEM)
    hbm = pl.BlockSpec(memory_space=pl.ANY)
    near, far, every = len(NEAR), len(RELAY), len(ALL)
    return pl.pallas_call(
        kernel,
        out_shape=jax.ShapeDtypeStruct((1, 5, 64, 64), F32),
        in_specs=[smem, smem, smem, hbm, hbm, hbm],
        out_specs=pl.BlockSpec(memory_space=pltpu.VMEM),
        scratch_shapes=[
            pltpu.SMEM((16,), jnp.int32),
            pltpu.VMEM((18, 3, 128, 128), BF),
            pltpu.VMEM((16, 3, 128, 128), BF),
            pltpu.VMEM((384, 384), BF),
            pltpu.VMEM((3, 128, 128), BF),
            pltpu.VMEM((6, 128, 64, 128), BF),
            pltpu.VMEM((6144, 128), F32),
            pltpu.VMEM((6144, 128), F32),
            pltpu.VMEM((2, 16, 16, 64, 128), BF),
            pltpu.VMEM((16, 16, AUX[0][1], 128), BF),
            pltpu.VMEM((16, 16, AUX[1][1], 128), BF),
            pltpu.VMEM((2, far, 8, 64, 128), BF),
            pltpu.VMEM((far, 8, AUX[0][1], 128), BF),
            pltpu.VMEM((far, 8, AUX[1][1], 128), BF),
            pltpu.VMEM((16, 16, 64, 128), BF),
            pltpu.VMEM((16, 16, 64, 128), BF),
            pltpu.VMEM((16, 64, 128), BF),
            pltpu.VMEM((16, 64, 128), BF),
            pltpu.VMEM((2, 16, 64, 128), BF),
            pltpu.VMEM((16, 64, 128), F32),
            pltpu.VMEM((16, 64, 128), F32),
            pltpu.VMEM((16, 32, 128), F32),
            pltpu.VMEM((64, 64), F32),
            dma((4, near)),
            dma((4, near)),
            dma((4, far)),
            dma((4, far)),
            dma((4, far)),
            dma((4, far)),
            dma((2,)),
            dma((2,)),
            dma((2, every)),
            dma((2, every)),
            dma((every,)),
            dma((every,)),
            dma((2,)),
            dma((2,)),
            dma((7,)),
            pltpu.SemaphoreType.REGULAR,
        ],
        compiler_params=pltpu.CompilerParams(
            collective_id=0, has_side_effects=True, vmem_limit_bytes=60 << 20
        ),
    )(slot_block, pair_kept, block_funcs, tensor_blocks, occupied, virtual)


def solution(mesh):
    placed = (
        P(("grp", "tp"), None, None, None, None),
        P("grp", None, None, None),
        P("grp", None, None, None),
        P("grp", None),
        P(),
        P(),
    )
    return jax.shard_map(
        body,
        mesh=mesh,
        in_specs=placed,
        out_specs=P(("grp", "tp"), None, None, None),
        check_vma=False,
    )
```

```python
import jax
import jax.numpy as jnp
from jax import lax
from jax.experimental import pallas as pl
from jax.experimental.pallas import tpu as pltpu
from jax.sharding import PartitionSpec as P

MESH = pl.DeviceIdType.MESH
BF = jnp.bfloat16
F32 = jnp.float32
SIDE = 4

NEAR = [(-1, -1), (1, 1), (1, -1), (-1, 1), (1, 0), (-1, 0), (0, 1), (0, -1)]
FAR = [(2, 0), (0, 2), (2, 1), (2, -1), (1, 2), (-1, 2), (2, 2)]
RELAY = []
for _dx, _dy in FAR:
    for _half, _sign in enumerate((1, -1)):
        _first = (_sign if _dx == 2 else _dx, _sign if _dy == 2 else _dy)
        RELAY.append((_first, (_dx - _first[0], _dy - _first[1]), _half))
ALL = NEAR + FAR
AUX = ((0, 48), (48, 16))


def place(dx, dy):
    me = lax.axis_index("tp")
    x = lax.rem(lax.rem(me, SIDE) + (dx + SIDE), SIDE)
    y = lax.rem(me // SIDE + (dy + SIDE), SIDE)
    return y * SIDE + x


def slice_of(tp):
    x, y = lax.rem(tp, SIDE), tp // SIDE
    return y * 2 + x // 2, lax.rem(x + y, 2)


def lanes(x):
    return jnp.concatenate([x[i] for i in range(x.shape[0])], axis=1)


def dot_nt(a, b):
    return lax.dot_general(a, b, (((1,), (1,)), ((), ())), preferred_element_type=F32)


def masked(block, row_limit, col_limit):
    row = lax.broadcasted_iota(jnp.int32, block.shape, 0)
    col = lax.broadcasted_iota(jnp.int32, block.shape, 1)
    return jnp.where((row < row_limit) & (col < col_limit), block.astype(F32), 0.0)


def kernel(
    slot_ref, kept_ref, funcs_ref, tensor, occupied, virtual, out,
    inv, oe, ve, ot, vd, kh, k32, h32, r01, r2a, r2b, rb, rba, rbb, zd, zu, ed, eu, es, pt, fin, dg, acc,
    near_s, near_r, one_s, one_r, two_s, two_r, edge_s, edge_r, fin_s, fin_r, dg_s, dg_r,
    halo_s, halo_r, loc, ready,
):
    me = lax.axis_index("tp")
    grp = lax.axis_index("grp")
    regions = lax.axis_size("grp")
    rows = 16
    kind = slice_of(me)[1]

    def dev(dx, dy):
        return (grp, place(dx, dy))

    def grp_at(step):
        return (lax.rem(grp + step + regions, regions), me)

    kt = tensor.at[0]
    region = occupied.shape[0]
    slab = funcs_ref.shape[0]
    first = grp * region
    loads = [
        pltpu.make_async_copy(occupied, oe.at[pl.ds(1, region)], loc.at[5]),
        pltpu.make_async_copy(kt, kh.at[pl.ds(0, 3)], loc.at[4]),
        pltpu.make_async_copy(virtual, ve, loc.at[6]),
    ]
    for c in loads:
        c.start()

    barrier = pltpu.get_barrier_semaphore()
    for dx, dy in NEAR:
        pl.semaphore_signal(barrier, inc=1, device_id=dev(dx, dy), device_id_type=MESH)
    pl.semaphore_signal(barrier, inc=1, device_id=grp_at(1), device_id_type=MESH)
    pl.semaphore_wait(barrier, len(NEAR) + 1)
    pl.semaphore_signal(ready, inc=1, device_id=grp_at(-1), device_id_type=MESH)

    def landing(slot, origin):
        return (r01.at[0, origin], r01.at[1, origin], r2a.at[origin], r2b.at[origin])[slot]

    def relayed(slot, i):
        return (rb.at[0, i], rb.at[1, i], rba.at[i], rbb.at[i])[slot]

    def source(slot, target, start, count, early=False):
        u, v = slice_of(target)
        part = pl.ds(u * rows + start, count)
        if slot == 0:
            return kt.at[v, part]
        if slot == 1 and early:
            return kt.at[2, part]
        if slot == 1:
            return kh.at[2 + 3 * v, part]
        return kh.at[4 - v, part, pl.ds(*AUX[slot - 2])]

    def send_far(slot, only=None):
        firsts = []
        for i, (hop, second, half) in enumerate(RELAY):
            target = place(hop[0] + second[0], hop[1] + second[1])
            c = pltpu.make_async_remote_copy(
                src_ref=source(slot, target, half * 8, 8, only == 0),
                dst_ref=relayed(slot, i),
                send_sem=one_s.at[slot, i],
                recv_sem=one_r.at[slot, i],
                device_id=dev(*hop),
                device_id_type=MESH,
            )
            if only is None:
                c.start()
            else:
                pl.when(slice_of(target)[1] == only)(c.start)
            firsts.append(c)
        return firsts

    def send_near(slot):
        nears = []
        for i, (dx, dy) in enumerate(NEAR):
            c = pltpu.make_async_remote_copy(
                src_ref=source(slot, place(dx, dy), 0, rows),
                dst_ref=landing(slot, me),
                send_sem=near_s.at[slot, i],
                recv_sem=near_r.at[slot, i],
                device_id=dev(dx, dy),
                device_id_type=MESH,
            )
            c.start()
            nears.append(c)
        own = pltpu.make_async_copy(source(slot, me, 0, rows), landing(slot, me), loc.at[slot])
        own.start()
        return nears, own

    def forward(slot, firsts):
        seconds = []
        for i, (hop, second, half) in enumerate(RELAY):
            firsts[i].wait_recv()
            c = pltpu.make_async_remote_copy(
                src_ref=relayed(slot, i),
                dst_ref=landing(slot, place(-hop[0], -hop[1])).at[pl.ds(half * 8, 8)],
                send_sem=two_s.at[slot, i],
                recv_sem=two_r.at[slot, i],
                device_id=dev(*second),
                device_id_type=MESH,
            )
            c.start()
            seconds.append(c)
        return seconds

    def arrive(nears, own, seconds):
        own.wait()
        for c in nears + seconds:
            c.wait_recv()

    firsts0 = send_far(0)
    send_far(1, 0)
    oe[0, 0] = jnp.zeros(oe.shape[2:], BF)
    oe[region + 1, 2] = jnp.zeros(oe.shape[2:], BF)

    def funcs(col):
        inside = (col >= 0) & (col < slab)
        return jnp.where(inside, funcs_ref[jnp.clip(col, 0, slab - 1)], 0)

    def bond(col):
        inside = (col >= 0) & (col < slab)
        return jnp.where(inside, kept_ref[jnp.clip(col, 0, slab - 1)], 0)

    def find(j, _):
        at = 0
        for k in range(region):
            at = jnp.where(slot_ref[0, k] == j, k, at)
        inv[j] = at
        return 0

    lax.fori_loop(0, region, find, 0)

    halos = []
    for i, (step, src, dst) in enumerate(
        (
            (-1, occupied.at[0, pl.ds(0, 2)], oe.at[region + 1, pl.ds(0, 2)]),
            (1, occupied.at[region - 1, pl.ds(1, 2)], oe.at[0, pl.ds(1, 2)]),
        )
    ):
        if step == 1:
            pl.semaphore_wait(ready, 1)
        c = pltpu.make_async_remote_copy(
            src_ref=src,
            dst_ref=dst,
            send_sem=halo_s.at[i],
            recv_sem=halo_r.at[i],
            device_id=grp_at(step),
            device_id_type=MESH,
        )
        c.start()
        halos.append(c)

    local = slot_ref[0, me]
    own_col = first + local
    around = [funcs(own_col - 1), funcs(own_col), funcs(own_col + 1)]
    rows_ok = [
        jnp.where(bond(own_col - 1) == 1, around[0], 0),
        around[1],
        jnp.where(bond(own_col) == 1, around[2], 0),
    ]
    loads[0].wait()
    for c in halos:
        c.wait_recv()
    for e in range(3):
        for d in range(3):
            if abs(d - e) > 1:
                block = jnp.zeros((128, 128), BF)
            else:
                block = masked(oe[local + e, d - e + 1], rows_ok[d], around[e]).T.astype(BF)
            ot[e * 128 : (e + 1) * 128, d * 128 : (d + 1) * 128] = block
    loads[1].wait()

    def half_chunk(i, _):
        cut = pl.ds(pl.multiple_of(i * 16, 16), 16)
        for d in range(3):
            k32[pl.ds(d * 2048, 2048), :] = kh[d, :, cut, :].reshape(2048, 128).astype(F32)
        for q in range(0, 16, 2):
            two = [k32[pl.ds(q + s, 384, stride=16), :] for s in range(2)]
            res = jnp.dot(
                ot[...], jnp.concatenate(two, axis=1).astype(BF), preferred_element_type=F32
            )
            for s in range(2):
                h32[pl.ds(q + s, 384, stride=16), :] = res[:, s * 128 : (s + 1) * 128]
        for e in range(3):
            kh[3 + e, :, cut, :] = h32[pl.ds(e * 2048, 2048), :].reshape(128, 16, 128).astype(BF)
        return 0

    lax.fori_loop(0, 4, half_chunk, 0)

    firsts1 = send_far(1, 1)
    firsts2 = send_far(2)
    firsts3 = send_far(3)
    seconds0 = forward(0, firsts0)
    seconds1 = forward(1, firsts1)
    nears0, own0 = send_near(0)
    nears1, own1 = send_near(1)
    seconds2 = forward(2, firsts2)
    nears2, own2 = send_near(2)
    seconds3 = forward(3, firsts3)
    nears3, own3 = send_near(3)
    loads[2].wait()
    for e in range(3):
        allowed = jnp.where(rows_ok[e] > 0, around[1], 0)
        vd[e] = masked(ve[local, 1], allowed, around[1]).astype(BF)
    acc[...] = jnp.zeros_like(acc)

    def own_part(i, _):
        e, cut = i // 8, pl.ds(lax.rem(i, 8) * 16, 16)
        z = jnp.dot(kh[e, cut].reshape(1024, 128), vd[e], preferred_element_type=F32)
        acc[...] += dot_nt(lanes(kh[3 + e, cut]), lanes(z.astype(BF).reshape(16, 64, 128)))
        return 0

    lax.fori_loop(0, 24, own_part, 0)
    dg[me] = jnp.concatenate([acc[:32], acc[32:]], axis=1)
    arrive(nears0, own0, seconds0)
    arrive(nears1, own1, seconds1)

    shares = []
    for i, (dx, dy) in enumerate(ALL):
        c = pltpu.make_async_remote_copy(
            src_ref=dg.at[me],
            dst_ref=dg.at[me],
            send_sem=dg_s.at[i],
            recv_sem=dg_r.at[i],
            device_id=dev(dx, dy),
            device_id_type=MESH,
        )
        c.start()
        shares.append(c)

    es[0] = r01[0, inv[0]]
    es[1] = r01[1 - kind, inv[15]]
    edges = []
    for i, (step, dst) in enumerate(((-1, ed), (1, eu))):
        c = pltpu.make_async_remote_copy(
            src_ref=es.at[i],
            dst_ref=dst,
            send_sem=edge_s.at[i],
            recv_sem=edge_r.at[i],
            device_id=grp_at(step),
            device_id_type=MESH,
        )
        c.start()
        edges.append(c)

    def times(block, j, side):
        col = first + j
        beside = funcs(col + side - 1)
        allowed = jnp.where((kind == 1) | (bond(col + side // 2 - 1) == 1), beside, 0)
        v = masked(ve[j, side], allowed, funcs(col)).astype(BF)
        z = jnp.dot(block.reshape(1024, 128), v, preferred_element_type=F32)
        return z.astype(BF).reshape(16, 64, 128)

    def other_part(j, _):
        zd[j] = times(r01[0, inv[j + 1]], j, 2)
        zu[j + 1] = times(r01[1 - kind, inv[j]], j + 1, 0)
        return 0

    lax.fori_loop(0, 15, other_part, 0)
    for c in edges:
        c.wait_recv()
    zd[15] = times(ed[...], 15, 2)
    zu[0] = times(eu[...], 0, 0)

    sums = []

    def finish(part, landed):
        start, count = AUX[part]
        cut = pl.ds(start, count)

        @pl.when(kind == 0)
        def _():
            def column(j, _):
                half = lanes(landed[inv[j]])
                pt[j, cut] = jnp.concatenate(
                    [dot_nt(half, lanes(zu[j])), dot_nt(half, lanes(zd[j]))], axis=1
                )
                return 0

            lax.fori_loop(0, 16, column, 0)

        @pl.when(kind == 1)
        def _():
            def column(j, _):
                pt[j, cut] = jnp.concatenate(
                    [
                        dot_nt(lanes(landed[inv[j]]), lanes(zu[j])),
                        dot_nt(lanes(r01[1, inv[j], :, cut]), lanes(zd[j])),
                    ],
                    axis=1,
                )
                return 0

            lax.fori_loop(0, 16, column, 0)

        for i, (dx, dy) in enumerate(ALL):
            c = pltpu.make_async_remote_copy(
                src_ref=pt.at[place(dx, dy), cut],
                dst_ref=fin.at[me, cut],
                send_sem=fin_s.at[part, i],
                recv_sem=fin_r.at[part, i],
                device_id=dev(dx, dy),
                device_id_type=MESH,
            )
            c.start()
            sums.append(c)

    arrive(nears2, own2, seconds2)
    finish(0, r2a)
    arrive(nears3, own3, seconds3)
    finish(1, r2b)
    fin[me] = pt[me]
    for c in shares + sums:
        c.wait_recv()
    scale = 1.0 / 128
    total = fin[0]
    for k in range(1, 16):
        total = total + fin[k]
    total = total * scale
    mid = dg[inv[me]] * scale
    out[0, 0] = jnp.zeros((64, 64), F32)
    out[0, 1] = total[:, :64]
    out[0, 2] = jnp.concatenate([mid[:, :64], mid[:, 64:]], axis=0)
    out[0, 3] = total[:, 64:]
    out[0, 4] = jnp.zeros((64, 64), F32)

    for c in firsts0 + firsts1 + firsts2 + firsts3 + nears0 + nears1 + nears2 + nears3:
        c.wait_send()
    for c in seconds0 + seconds1 + seconds2 + seconds3 + halos + edges + shares + sums:
        c.wait_send()


def body(tensor_blocks, occupied, virtual, slot_block, pair_kept, block_funcs):
    dma = pltpu.SemaphoreType.DMA
    smem = pl.BlockSpec(memory_space=pltpu.SMEM)
    hbm = pl.BlockSpec(memory_space=pl.ANY)
    near, far, every = len(NEAR), len(RELAY), len(ALL)
    return pl.pallas_call(
        kernel,
        out_shape=jax.ShapeDtypeStruct((1, 5, 64, 64), F32),
        in_specs=[smem, smem, smem, hbm, hbm, hbm],
        out_specs=pl.BlockSpec(memory_space=pltpu.VMEM),
        scratch_shapes=[
            pltpu.SMEM((16,), jnp.int32),
            pltpu.VMEM((18, 3, 128, 128), BF),
            pltpu.VMEM((16, 3, 128, 128), BF),
            pltpu.VMEM((384, 384), BF),
            pltpu.VMEM((3, 128, 128), BF),
            pltpu.VMEM((6, 128, 64, 128), BF),
            pltpu.VMEM((6144, 128), F32),
            pltpu.VMEM((6144, 128), F32),
            pltpu.VMEM((2, 16, 16, 64, 128), BF),
            pltpu.VMEM((16, 16, AUX[0][1], 128), BF),
            pltpu.VMEM((16, 16, AUX[1][1], 128), BF),
            pltpu.VMEM((2, far, 8, 64, 128), BF),
            pltpu.VMEM((far, 8, AUX[0][1], 128), BF),
            pltpu.VMEM((far, 8, AUX[1][1], 128), BF),
            pltpu.VMEM((16, 16, 64, 128), BF),
            pltpu.VMEM((16, 16, 64, 128), BF),
            pltpu.VMEM((16, 64, 128), BF),
            pltpu.VMEM((16, 64, 128), BF),
            pltpu.VMEM((2, 16, 64, 128), BF),
            pltpu.VMEM((16, 64, 128), F32),
            pltpu.VMEM((16, 64, 128), F32),
            pltpu.VMEM((16, 32, 128), F32),
            pltpu.VMEM((64, 64), F32),
            dma((4, near)),
            dma((4, near)),
            dma((4, far)),
            dma((4, far)),
            dma((4, far)),
            dma((4, far)),
            dma((2,)),
            dma((2,)),
            dma((2, every)),
            dma((2, every)),
            dma((every,)),
            dma((every,)),
            dma((2,)),
            dma((2,)),
            dma((7,)),
            pltpu.SemaphoreType.REGULAR,
        ],
        compiler_params=pltpu.CompilerParams(
            collective_id=0, has_side_effects=True, vmem_limit_bytes=60 << 20
        ),
    )(slot_block, pair_kept, block_funcs, tensor_blocks, occupied, virtual)


def solution(mesh):
    placed = (
        P(("grp", "tp"), None, None, None, None),
        P("grp", None, None, None),
        P("grp", None, None, None),
        P("grp", None),
        P(),
        P(),
    )
    return jax.shard_map(
        body,
        mesh=mesh,
        in_specs=placed,
        out_specs=P(("grp", "tp"), None, None, None),
        check_vma=False,
    )
```

```python
import jax
import jax.numpy as jnp
from jax import lax
from jax.experimental import pallas as pl
from jax.experimental.pallas import tpu as pltpu
from jax.sharding import PartitionSpec as P

MESH = pl.DeviceIdType.MESH
BF = jnp.bfloat16
F32 = jnp.float32
SIDE = 4

NEAR = [(-1, -1), (1, 1), (1, -1), (-1, 1), (0, 1), (0, -1), (1, 0), (-1, 0)]
FAR = [(2, 0), (0, 2), (2, 1), (2, -1), (1, 2), (-1, 2), (2, 2)]
RELAY = []
for _dx, _dy in FAR:
    for _half, _sign in enumerate((1, -1)):
        _first = (_sign if _dx == 2 else _dx, _sign if _dy == 2 else _dy)
        RELAY.append((_first, (_dx - _first[0], _dy - _first[1]), _half))
ALL = NEAR + FAR
AUX = ((0, 48), (48, 16))


def place(dx, dy):
    me = lax.axis_index("tp")
    x = lax.rem(lax.rem(me, SIDE) + (dx + SIDE), SIDE)
    y = lax.rem(me // SIDE + (dy + SIDE), SIDE)
    return y * SIDE + x


def slice_of(tp):
    x, y = lax.rem(tp, SIDE), tp // SIDE
    return y * 2 + x // 2, lax.rem(x + y, 2)


def lanes(x):
    return jnp.concatenate([x[i] for i in range(x.shape[0])], axis=1)


def dot_nt(a, b):
    return lax.dot_general(a, b, (((1,), (1,)), ((), ())), preferred_element_type=F32)


def masked(block, row_limit, col_limit):
    row = lax.broadcasted_iota(jnp.int32, block.shape, 0)
    col = lax.broadcasted_iota(jnp.int32, block.shape, 1)
    return jnp.where((row < row_limit) & (col < col_limit), block.astype(F32), 0.0)


def kernel(
    slot_ref, kept_ref, funcs_ref, tensor, occupied, virtual, out,
    inv, oe, ve, ot, vd, kh, k32, h32, r01, r2a, r2b, rb, rba, rbb, zd, zu, ed, eu, es, pt, fin, dg, acc,
    near_s, near_r, one_s, one_r, two_s, two_r, edge_s, edge_r, fin_s, fin_r, dg_s, dg_r,
    halo_s, halo_r, loc, ready,
):
    me = lax.axis_index("tp")
    grp = lax.axis_index("grp")
    regions = lax.axis_size("grp")
    rows = 16
    kind = slice_of(me)[1]

    def dev(dx, dy):
        return (grp, place(dx, dy))

    def grp_at(step):
        return (lax.rem(grp + step + regions, regions), me)

    kt = tensor.at[0]
    region = occupied.shape[0]
    slab = funcs_ref.shape[0]
    first = grp * region
    loads = [
        pltpu.make_async_copy(occupied, oe.at[pl.ds(1, region)], loc.at[5]),
        pltpu.make_async_copy(kt, kh.at[pl.ds(0, 3)], loc.at[4]),
        pltpu.make_async_copy(virtual, ve, loc.at[6]),
    ]
    for c in loads:
        c.start()

    barrier = pltpu.get_barrier_semaphore()
    for dx, dy in NEAR:
        pl.semaphore_signal(barrier, inc=1, device_id=dev(dx, dy), device_id_type=MESH)
    pl.semaphore_signal(barrier, inc=1, device_id=grp_at(1), device_id_type=MESH)
    pl.semaphore_wait(barrier, len(NEAR) + 1)
    pl.semaphore_signal(ready, inc=1, device_id=grp_at(-1), device_id_type=MESH)

    def landing(slot, origin):
        return (r01.at[0, origin], r01.at[1, origin], r2a.at[origin], r2b.at[origin])[slot]

    def relayed(slot, i):
        return (rb.at[0, i], rb.at[1, i], rba.at[i], rbb.at[i])[slot]

    def source(slot, target, start, count, early=False):
        u, v = slice_of(target)
        part = pl.ds(u * rows + start, count)
        if slot == 0:
            return kt.at[v, part]
        if slot == 1 and early:
            return kt.at[2, part]
        if slot == 1:
            return kh.at[2 + 3 * v, part]
        return kh.at[4 - v, part, pl.ds(*AUX[slot - 2])]

    def send_far(slot, only=None):
        firsts = []
        for i, (hop, second, half) in enumerate(RELAY):
            target = place(hop[0] + second[0], hop[1] + second[1])
            c = pltpu.make_async_remote_copy(
                src_ref=source(slot, target, half * 8, 8, only == 0),
                dst_ref=relayed(slot, i),
                send_sem=one_s.at[slot, i],
                recv_sem=one_r.at[slot, i],
                device_id=dev(*hop),
                device_id_type=MESH,
            )
            if only is None:
                c.start()
            else:
                pl.when(slice_of(target)[1] == only)(c.start)
            firsts.append(c)
        return firsts

    def send_near(slot):
        nears = []
        for i, (dx, dy) in enumerate(NEAR):
            c = pltpu.make_async_remote_copy(
                src_ref=source(slot, place(dx, dy), 0, rows),
                dst_ref=landing(slot, me),
                send_sem=near_s.at[slot, i],
                recv_sem=near_r.at[slot, i],
                device_id=dev(dx, dy),
                device_id_type=MESH,
            )
            c.start()
            nears.append(c)
        own = pltpu.make_async_copy(source(slot, me, 0, rows), landing(slot, me), loc.at[slot])
        own.start()
        return nears, own

    def forward(slot, firsts):
        seconds = []
        for i, (hop, second, half) in enumerate(RELAY):
            firsts[i].wait_recv()
            c = pltpu.make_async_remote_copy(
                src_ref=relayed(slot, i),
                dst_ref=landing(slot, place(-hop[0], -hop[1])).at[pl.ds(half * 8, 8)],
                send_sem=two_s.at[slot, i],
                recv_sem=two_r.at[slot, i],
                device_id=dev(*second),
                device_id_type=MESH,
            )
            c.start()
            seconds.append(c)
        return seconds

    def arrive(nears, own, seconds):
        own.wait()
        for c in nears + seconds:
            c.wait_recv()

    firsts0 = send_far(0)
    send_far(1, 0)
    oe[0, 0] = jnp.zeros(oe.shape[2:], BF)
    oe[region + 1, 2] = jnp.zeros(oe.shape[2:], BF)

    def funcs(col):
        inside = (col >= 0) & (col < slab)
        return jnp.where(inside, funcs_ref[jnp.clip(col, 0, slab - 1)], 0)

    def bond(col):
        inside = (col >= 0) & (col < slab)
        return jnp.where(inside, kept_ref[jnp.clip(col, 0, slab - 1)], 0)

    def find(j, _):
        at = 0
        for k in range(region):
            at = jnp.where(slot_ref[0, k] == j, k, at)
        inv[j] = at
        return 0

    lax.fori_loop(0, region, find, 0)

    halos = []
    for i, (step, src, dst) in enumerate(
        (
            (-1, occupied.at[0, pl.ds(0, 2)], oe.at[region + 1, pl.ds(0, 2)]),
            (1, occupied.at[region - 1, pl.ds(1, 2)], oe.at[0, pl.ds(1, 2)]),
        )
    ):
        if step == 1:
            pl.semaphore_wait(ready, 1)
        c = pltpu.make_async_remote_copy(
            src_ref=src,
            dst_ref=dst,
            send_sem=halo_s.at[i],
            recv_sem=halo_r.at[i],
            device_id=grp_at(step),
            device_id_type=MESH,
        )
        c.start()
        halos.append(c)

    local = slot_ref[0, me]
    own_col = first + local
    around = [funcs(own_col - 1), funcs(own_col), funcs(own_col + 1)]
    rows_ok = [
        jnp.where(bond(own_col - 1) == 1, around[0], 0),
        around[1],
        jnp.where(bond(own_col) == 1, around[2], 0),
    ]
    loads[0].wait()
    for c in halos:
        c.wait_recv()
    for e in range(3):
        for d in range(3):
            if abs(d - e) > 1:
                block = jnp.zeros((128, 128), BF)
            else:
                block = masked(oe[local + e, d - e + 1], rows_ok[d], around[e]).T.astype(BF)
            ot[e * 128 : (e + 1) * 128, d * 128 : (d + 1) * 128] = block
    loads[1].wait()

    def half_chunk(i, _):
        cut = pl.ds(pl.multiple_of(i * 16, 16), 16)
        for d in range(3):
            k32[pl.ds(d * 2048, 2048), :] = kh[d, :, cut, :].reshape(2048, 128).astype(F32)
        for q in range(0, 16, 2):
            two = [k32[pl.ds(q + s, 384, stride=16), :] for s in range(2)]
            res = jnp.dot(
                ot[...], jnp.concatenate(two, axis=1).astype(BF), preferred_element_type=F32
            )
            for s in range(2):
                h32[pl.ds(q + s, 384, stride=16), :] = res[:, s * 128 : (s + 1) * 128]
        for e in range(3):
            kh[3 + e, :, cut, :] = h32[pl.ds(e * 2048, 2048), :].reshape(128, 16, 128).astype(BF)
        return 0

    lax.fori_loop(0, 4, half_chunk, 0)

    firsts1 = send_far(1, 1)
    firsts2 = send_far(2)
    firsts3 = send_far(3)
    seconds0 = forward(0, firsts0)
    seconds1 = forward(1, firsts1)
    nears0, own0 = send_near(0)
    nears1, own1 = send_near(1)
    seconds2 = forward(2, firsts2)
    nears2, own2 = send_near(2)
    seconds3 = forward(3, firsts3)
    nears3, own3 = send_near(3)
    loads[2].wait()
    for e in range(3):
        allowed = jnp.where(rows_ok[e] > 0, around[1], 0)
        vd[e] = masked(ve[local, 1], allowed, around[1]).astype(BF)
    acc[...] = jnp.zeros_like(acc)

    def own_part(i, _):
        e, cut = i // 8, pl.ds(lax.rem(i, 8) * 16, 16)
        z = jnp.dot(kh[e, cut].reshape(1024, 128), vd[e], preferred_element_type=F32)
        acc[...] += dot_nt(lanes(kh[3 + e, cut]), lanes(z.astype(BF).reshape(16, 64, 128)))
        return 0

    lax.fori_loop(0, 24, own_part, 0)
    dg[me] = jnp.concatenate([acc[:32], acc[32:]], axis=1)
    arrive(nears0, own0, seconds0)
    arrive(nears1, own1, seconds1)

    shares = []
    for i, (dx, dy) in enumerate(ALL):
        c = pltpu.make_async_remote_copy(
            src_ref=dg.at[me],
            dst_ref=dg.at[me],
            send_sem=dg_s.at[i],
            recv_sem=dg_r.at[i],
            device_id=dev(dx, dy),
            device_id_type=MESH,
        )
        c.start()
        shares.append(c)

    es[0] = r01[0, inv[0]]
    es[1] = r01[1 - kind, inv[15]]
    edges = []
    for i, (step, dst) in enumerate(((-1, ed), (1, eu))):
        c = pltpu.make_async_remote_copy(
            src_ref=es.at[i],
            dst_ref=dst,
            send_sem=edge_s.at[i],
            recv_sem=edge_r.at[i],
            device_id=grp_at(step),
            device_id_type=MESH,
        )
        c.start()
        edges.append(c)

    def times(block, j, side):
        col = first + j
        beside = funcs(col + side - 1)
        allowed = jnp.where((kind == 1) | (bond(col + side // 2 - 1) == 1), beside, 0)
        v = masked(ve[j, side], allowed, funcs(col)).astype(BF)
        z = jnp.dot(block.reshape(1024, 128), v, preferred_element_type=F32)
        return z.astype(BF).reshape(16, 64, 128)

    def other_part(j, _):
        zd[j] = times(r01[0, inv[j + 1]], j, 2)
        zu[j + 1] = times(r01[1 - kind, inv[j]], j + 1, 0)
        return 0

    lax.fori_loop(0, 15, other_part, 0)
    for c in edges:
        c.wait_recv()
    zd[15] = times(ed[...], 15, 2)
    zu[0] = times(eu[...], 0, 0)

    sums = []

    def finish(part, landed):
        start, count = AUX[part]
        cut = pl.ds(start, count)

        @pl.when(kind == 0)
        def _():
            def column(j, _):
                half = lanes(landed[inv[j]])
                pt[j, cut] = jnp.concatenate(
                    [dot_nt(half, lanes(zu[j])), dot_nt(half, lanes(zd[j]))], axis=1
                )
                return 0

            lax.fori_loop(0, 16, column, 0)

        @pl.when(kind == 1)
        def _():
            def column(j, _):
                pt[j, cut] = jnp.concatenate(
                    [
                        dot_nt(lanes(landed[inv[j]]), lanes(zu[j])),
                        dot_nt(lanes(r01[1, inv[j], :, cut]), lanes(zd[j])),
                    ],
                    axis=1,
                )
                return 0

            lax.fori_loop(0, 16, column, 0)

        for i, (dx, dy) in enumerate(ALL):
            c = pltpu.make_async_remote_copy(
                src_ref=pt.at[place(dx, dy), cut],
                dst_ref=fin.at[me, cut],
                send_sem=fin_s.at[part, i],
                recv_sem=fin_r.at[part, i],
                device_id=dev(dx, dy),
                device_id_type=MESH,
            )
            c.start()
            sums.append(c)

    arrive(nears2, own2, seconds2)
    finish(0, r2a)
    arrive(nears3, own3, seconds3)
    finish(1, r2b)
    fin[me] = pt[me]
    for c in shares + sums:
        c.wait_recv()
    scale = 1.0 / 128
    total = fin[0]
    for k in range(1, 16):
        total = total + fin[k]
    total = total * scale
    mid = dg[inv[me]] * scale
    out[0, 0] = jnp.zeros((64, 64), F32)
    out[0, 1] = total[:, :64]
    out[0, 2] = jnp.concatenate([mid[:, :64], mid[:, 64:]], axis=0)
    out[0, 3] = total[:, 64:]
    out[0, 4] = jnp.zeros((64, 64), F32)

    for c in firsts0 + firsts1 + firsts2 + firsts3 + nears0 + nears1 + nears2 + nears3:
        c.wait_send()
    for c in seconds0 + seconds1 + seconds2 + seconds3 + halos + edges + shares + sums:
        c.wait_send()


def body(tensor_blocks, occupied, virtual, slot_block, pair_kept, block_funcs):
    dma = pltpu.SemaphoreType.DMA
    smem = pl.BlockSpec(memory_space=pltpu.SMEM)
    hbm = pl.BlockSpec(memory_space=pl.ANY)
    near, far, every = len(NEAR), len(RELAY), len(ALL)
    return pl.pallas_call(
        kernel,
        out_shape=jax.ShapeDtypeStruct((1, 5, 64, 64), F32),
        in_specs=[smem, smem, smem, hbm, hbm, hbm],
        out_specs=pl.BlockSpec(memory_space=pltpu.VMEM),
        scratch_shapes=[
            pltpu.SMEM((16,), jnp.int32),
            pltpu.VMEM((18, 3, 128, 128), BF),
            pltpu.VMEM((16, 3, 128, 128), BF),
            pltpu.VMEM((384, 384), BF),
            pltpu.VMEM((3, 128, 128), BF),
            pltpu.VMEM((6, 128, 64, 128), BF),
            pltpu.VMEM((6144, 128), F32),
            pltpu.VMEM((6144, 128), F32),
            pltpu.VMEM((2, 16, 16, 64, 128), BF),
            pltpu.VMEM((16, 16, AUX[0][1], 128), BF),
            pltpu.VMEM((16, 16, AUX[1][1], 128), BF),
            pltpu.VMEM((2, far, 8, 64, 128), BF),
            pltpu.VMEM((far, 8, AUX[0][1], 128), BF),
            pltpu.VMEM((far, 8, AUX[1][1], 128), BF),
            pltpu.VMEM((16, 16, 64, 128), BF),
            pltpu.VMEM((16, 16, 64, 128), BF),
            pltpu.VMEM((16, 64, 128), BF),
            pltpu.VMEM((16, 64, 128), BF),
            pltpu.VMEM((2, 16, 64, 128), BF),
            pltpu.VMEM((16, 64, 128), F32),
            pltpu.VMEM((16, 64, 128), F32),
            pltpu.VMEM((16, 32, 128), F32),
            pltpu.VMEM((64, 64), F32),
            dma((4, near)),
            dma((4, near)),
            dma((4, far)),
            dma((4, far)),
            dma((4, far)),
            dma((4, far)),
            dma((2,)),
            dma((2,)),
            dma((2, every)),
            dma((2, every)),
            dma((every,)),
            dma((every,)),
            dma((2,)),
            dma((2,)),
            dma((7,)),
            pltpu.SemaphoreType.REGULAR,
        ],
        compiler_params=pltpu.CompilerParams(
            collective_id=0, has_side_effects=True, vmem_limit_bytes=60 << 20
        ),
    )(slot_block, pair_kept, block_funcs, tensor_blocks, occupied, virtual)


def solution(mesh):
    placed = (
        P(("grp", "tp"), None, None, None, None),
        P("grp", None, None, None),
        P("grp", None, None, None),
        P("grp", None),
        P(),
        P(),
    )
    return jax.shard_map(
        body,
        mesh=mesh,
        in_specs=placed,
        out_specs=P(("grp", "tp"), None, None, None),
        check_vma=False,
    )
```
